256 devices in a mesh: zone: 8 (over x, core), sub: 8 (over z), row: 4 (over y).
Axes of the slice: x: 4, y: 4, z: 8, core: 2. Of those that a mesh axis runs over, the one named last changes fastest.
Arguments:
- z_inverse: bfloat16 [64, 2048, 2048], P(('zone', 'sub'), 'row'), may hold values from -2 to 2
- sources: bfloat16 [4, 64, 2048, 512], P(None, ('zone', 'sub'), 'row'), may hold values from -6 to 6
- v_start: float32 [64, 2048, 512], P(('zone', 'sub'), 'row'), may hold values from -6 to 6
- hist_near: float32 [2, 64, 256, 512], P(None, ('zone', 'sub'), 'row'), may hold values from -6 to 6
- hist_far: float32 [2, 64, 256, 512], P(None, ('zone', 'sub'), 'row'), may hold values from -6 to 6
- switch_on: int32 [4, 64, 2048], P(None, ('zone', 'sub'), 'row'), may hold values 0 or 1
- switch_cond: float32 [64, 2048], P(('zone', 'sub'), 'row'), may hold values from 0.1 to 1
- fault_node: int32 [512], replicated, may hold values from 0 to 2047
- fault_cond: float32 [512], replicated, may hold values from 0.2 to 1.5
- remote_sub: int32 [64, 256, 1], P(('zone', 'sub'), 'row'), may hold values from 0 to 63; in each aligned block of 64 rows (0 to 63, 64 to 127, ..., all dimensions but the last counted through in order) at most 2 rows name the same one
- near_node: int32 [64, 256], P(('zone', 'sub'), 'row'), may hold values from 0 to 511
- far_node: int32 [64, 256], P(('zone', 'sub'), 'row'), may hold values from 0 to 511
- line_gain: float32 [64, 256], P(('zone', 'sub'), 'row'), may hold values from 0.3 to 1.5
Outputs:
- v_last: float32 [64, 2048, 512], P(('zone', 'sub'), 'row')
The draws below stay inside these ranges and needn't reach their ends.
All inputs are finite; a program needn't handle non-finite values. No bound on the sum of `switch_on` on one device may be relied on, other than what follows from the above.
Results may differ from the reference program's by a relative error of at most 0.0034.
Values may be sent and summed in bfloat16 or wider, within the bound.
A program may use at most 64 MiB of HBM per device.

```python
import math
import jax
import jax.numpy as jnp
import numpy as np
from jax import lax

NODES = 2048
CASES = 512
LINES_ROW = 64
STEPS = 4
SUBS = 64
LINES_SUB = 256
CAP = 2
N_ROW = 4


def draw_z_inverse(key, part):
    key = jax.random.fold_in(key, 11)
    first, second = jax.random.split(key)
    spread = jax.random.normal(first, (SUBS, NODES, NODES), jnp.float32) * (0.5 / NODES ** 0.5)
    spread = jnp.clip(spread, -0.5, 0.5)
    diagonal = jax.random.uniform(second, (SUBS, NODES, 1), jnp.float32, 0.6, 1.2)
    places = jnp.arange(NODES, dtype=jnp.int32)
    identity = places[:, None] == places[None, :]
    return jnp.where(identity[None], diagonal, spread).astype(jnp.bfloat16)


def touch_ends(entries, own_key, smallest, high):
    longest = entries.shape.index(max(entries.shape))
    spots = []
    for shift in (0, 1):
        where = [jax.random.randint(jax.random.fold_in(own_key, axis), (), 0, length) for axis, length in enumerate(entries.shape)]
        where[longest] = (where[longest] + shift) % entries.shape[longest]
        spots.append(tuple(where))
    return entries.at[spots[0]].set(smallest).at[spots[1]].set(high)


def shard_levels(rng, dims, cuts, least, high):
    def one(position, blocks):
        draws = jax.random.uniform(jax.random.fold_in(jax.random.fold_in(rng, 6), position), (blocks,), jnp.float32, least / len(cuts), high / len(cuts))
        return jnp.repeat(jnp.exp(draws), dims[position] // blocks).reshape((-1,) + (1,) * (len(dims) - position - 1))

    level = one(*cuts[0])
    for cut in cuts[1:]:
        level = level * one(*cut)
    return level


def shared_out(own_key, own, number, rows, amount, top, reach, slope):
    order = jax.random.permutation(own_key, amount)
    packed, ordinary = portions_of(amount, rows * top, reach, slope, True), portions_of(amount, rows * top, reach, slope, False)
    places = jnp.arange(amount)

    def named(tallies, rotation):
        used = int((tallies > 0).sum())
        fixed = max(1, used // 4)
        moved = fixed + (places - fixed + rotation * (used - fixed)) % max(1, amount - fixed)
        return jnp.zeros((amount,), jnp.int32).at[order[jnp.where(places < fixed, places, moved)]].set(jnp.asarray(tallies, jnp.int32))

    tallies = jnp.where(number % 4 == 0, named(packed, number // 4), named(ordinary, number - number // 4 - 1))
    mixed = jax.random.permutation(jax.random.fold_in(own, 3), amount)
    source_of, sink = mixed[0:amount // 2 * 2:2], mixed[1:amount // 2 * 2:2]
    margin = jnp.minimum(tallies[source_of] - 1, reach - tallies[sink]) // 2
    margin = jnp.where((source_of == order[0]) | (sink == order[0]) | (tallies[sink] == 0), 0, jnp.maximum(margin, 0))
    moved = jax.random.randint(jax.random.fold_in(own, 4), (amount // 2,), 0, 1 << 20) % (margin + 1)
    tallies = tallies.at[source_of].add(-moved).at[sink].add(moved)
    items = jnp.searchsorted(jnp.cumsum(tallies), jnp.arange(rows * top), side="right").astype(jnp.int32)
    grid = items.reshape(top, rows).T
    grid = grid[jax.random.permutation(jax.random.fold_in(own, 1), rows)]
    rotation = jax.random.randint(jax.random.fold_in(own, 2), (rows, 1), 0, top)
    return jnp.take_along_axis(grid, (jnp.arange(top)[None, :] + rotation) % top, axis=1)


def portions_of(amount, total, limit, lean, full):
    portions = [(1 << 20) // math.isqrt(grade ** lean) + 1 for grade in range(1, amount + 1)]
    largest = limit if full else min(limit, max(-(-total // amount), total * portions[0] // sum(portions)))
    least = 1 if total - largest >= amount - 1 else 0
    holding, surplus = [largest] + [least] * (amount - 1), total - largest - least * (amount - 1)
    while surplus > 0:
        candidates = [i for i in range(1, amount) if holding[i] < largest] or [i for i in range(1, amount) if holding[i] < limit]
        pool, left = sum([portions[i] for i in candidates]), surplus
        for i in candidates:
            more = min(limit - holding[i], max(1, left * portions[i] // pool), surplus)
            holding[i] = holding[i] + more
            surplus = surplus - more
    return np.array(holding)


def noise(stream_key, shape, width, reach, cuts=(), held_as=jnp.bfloat16):
    result = jax.random.normal(stream_key, shape, jnp.float32) * width
    if len(cuts) > 0:
        result = shard_levels(stream_key, shape, cuts, -0.22, 0.18) * result
    return jnp.clip(result, min=-reach, max=reach).astype(held_as)


def setup_inputs(seed: int = 0) -> dict:
    splits = jax.random.split(jax.random.key(seed), 14)
    z_inverse = draw_z_inverse(jax.random.fold_in(splits[13], 71), 0)
    sources = noise(splits[1], (STEPS, SUBS, NODES, CASES), 1.0, 6.0, ((1, 64), (2, 4)))
    v_start = noise(splits[2], (SUBS, NODES, CASES), 1.0, 6.0, ((0, 64), (1, 4)), jnp.float32)
    hist_near = noise(splits[3], (2, SUBS, LINES_SUB, CASES), 1.0, 6.0, ((1, 64), (2, 4)), jnp.float32)
    hist_far = noise(splits[4], (2, SUBS, LINES_SUB, CASES), 1.0, 6.0, ((1, 64), (2, 4)), jnp.float32)
    switch_on = touch_ends((jax.random.randint(splits[5], (STEPS, SUBS, NODES), 0, 2) < 1).astype(jnp.int32), jax.random.fold_in(splits[5], 1), 0, 1)
    switch_cond = jnp.clip(jnp.exp(math.log(1.0) - 2.3025851 * jax.random.uniform(splits[6], (SUBS, NODES), jnp.float32) ** shard_levels(splits[6], (SUBS, NODES), ((0, 64), (1, 4)), -0.2, 0.2)), 0.1, 1.0)
    fault_node = touch_ends(jax.random.randint(splits[7], (CASES,), 0, NODES), jax.random.fold_in(splits[7], 1), 0, NODES - 1).astype(jnp.int32)
    fault_cond = jnp.clip(jnp.exp(jax.random.uniform(splits[8], (CASES,), jnp.float32, math.log(0.2), math.log(1.5))), 0.2, 1.5)
    remote_sub_keys = jax.random.split(jax.random.fold_in(splits[9], 1), SUBS * LINES_SUB // LINES_ROW)
    remote_sub_turns = jax.random.permutation(jax.random.fold_in(splits[9], 3), SUBS * LINES_SUB // LINES_ROW)
    remote_sub = jax.vmap(lambda own, number: shared_out(jax.random.fold_in(splits[9], 2), own, number, LINES_ROW, SUBS, 1, CAP, 2))(remote_sub_keys, remote_sub_turns).reshape((SUBS, LINES_SUB, 1))
    near_node = touch_ends(jax.random.randint(splits[10], (SUBS, LINES_SUB), 0, NODES // N_ROW), jax.random.fold_in(splits[10], 1), 0, (NODES // N_ROW) - 1).astype(jnp.int32)
    far_node = touch_ends(jax.random.randint(splits[11], (SUBS, LINES_SUB), 0, NODES // N_ROW), jax.random.fold_in(splits[11], 1), 0, (NODES // N_ROW) - 1).astype(jnp.int32)
    line_gain = jnp.clip(jnp.exp(math.log(1.5) - 1.60943787 * jax.random.uniform(splits[12], (SUBS, LINES_SUB), jnp.float32) ** shard_levels(splits[12], (SUBS, LINES_SUB), ((0, 64), (1, 4)), -0.2, 0.2)), 0.3, 1.5)
    return dict(z_inverse=z_inverse, sources=sources, v_start=v_start, hist_near=hist_near, hist_far=hist_far, switch_on=switch_on, switch_cond=switch_cond, fault_node=fault_node, fault_cond=fault_cond, remote_sub=remote_sub, near_node=near_node, far_node=far_node, line_gain=line_gain)


def solve_all(z_inverse, injb):
    def one(pair):
        return jnp.dot(pair[0].astype(jnp.float32), pair[1].astype(jnp.float32), precision=lax.Precision.HIGHEST)
    return lax.map(one, (z_inverse, injb))


def reference(z_inverse, sources, v_start, hist_near, hist_far, switch_on, switch_cond, fault_node, fault_cond, remote_sub, near_node, far_node, line_gain):
    block = NODES // N_ROW
    offset = (jnp.arange(LINES_SUB, dtype=jnp.int32) // LINES_ROW) * block
    node_a = near_node + offset[None, :]
    node_b = far_node + offset[None, :]
    target = remote_sub[:, :, 0]
    owner = jnp.broadcast_to(jnp.arange(SUBS, dtype=jnp.int32)[:, None], node_a.shape)
    gain = line_gain[:, :, None]
    fault_mask = (jnp.arange(NODES, dtype=jnp.int32)[:, None] == fault_node[None, :]).astype(jnp.float32)
    fault_term = fault_mask * fault_cond[None, :]
    v_prev = v_start
    near_list, far_list, vn_list, vf_list = [], [], [], []
    for step in range(STEPS):
        if step < 2:
            near_h = hist_near[step]
            far_h = hist_far[step]
        else:
            far_h = gain * vn_list[step - 2] - near_list[step - 2]
            near_h = gain * vf_list[step - 2] - far_list[step - 2]
        near_list.append(near_h)
        far_list.append(far_h)
        lines_in = jnp.zeros((SUBS, NODES, CASES), jnp.float32).at[owner, node_a].add(near_h).at[target, node_b].add(far_h)
        switched = switch_on[step].astype(jnp.float32) * switch_cond
        inj = sources[step].astype(jnp.float32) + lines_in - switched[:, :, None] * v_prev - fault_term[None] * v_prev
        injb = inj.astype(jnp.bfloat16)
        volts = solve_all(z_inverse, injb)
        vn_list.append(volts[owner, node_a])
        vf_list.append(volts[target, node_b])
        v_prev = volts
    return v_prev
```

```python
import functools

import jax
import jax.numpy as jnp
from jax import lax
from jax.experimental import pallas as pl
from jax.experimental.pallas import tpu as pltpu
from jax.sharding import PartitionSpec as P

MESH = pl.DeviceIdType.MESH
F32 = jnp.float32
BF16 = jnp.bfloat16
GROUPS = 4
AHEAD = 1


def dot(a, b):
    return jnp.dot(a, b, preferred_element_type=F32)


def iota(shape, dim):
    return lax.broadcasted_iota(jnp.int32, shape, dim)


def one_hot(mask):
    return jnp.where(mask, 1.0, 0.0).astype(BF16)


def to_column(row, size):
    eye = iota((size, size), 0) == iota((size, size), 1)
    return jnp.sum(jnp.where(eye, row, 0.0), axis=1, keepdims=True)


def to_row(column, size):
    eye = iota((size, size), 0) == iota((size, size), 1)
    return jnp.sum(jnp.where(eye, column, 0.0), axis=0, keepdims=True)


def kernel(
    zones,
    subs,
    z_hbm,
    src_hbm,
    vs_hbm,
    near_hbm,
    far_hbm,
    switch_on,
    switch_cond,
    fault_node,
    fault_cond,
    remote_sub,
    near_node,
    far_node,
    line_gain,
    out_hbm,
    zr,
    x,
    v,
    src,
    hist_near,
    hist_far,
    switched,
    scatter,
    gather,
    slots_out,
    slots_back,
    swap,
    gain,
    rhs,
    oa0,
    ra0,
    ob0,
    rb0,
    oa1,
    ra1,
    ob1,
    rb1,
    oa2,
    ra2,
    ob2,
    rb2,
    oa,
    ra,
    ob,
    rb,
    load_sem,
    send_sem,
    left_sem,
    right_sem,
    far_sem,
    ex_send,
    ex_recv,
    out_sem,
):
    rows, nodes = z_hbm.shape
    steps, _, cases = src_hbm.shape
    lines = near_node.shape[1]
    slots = 2 * zones * subs
    block_a, block_b = 2 * zones, 2 * subs
    width = cases // GROUPS
    half = 2 * width
    items = steps * GROUPS
    my_zone, my_sub, me = (lax.axis_index(name) for name in ("zone", "sub", "row"))
    right, left, across = lax.rem(me + 1, 4), lax.rem(me + 3, 4), lax.rem(me + 2, 4)

    loads = [pltpu.make_async_copy(far_hbm, hist_far, load_sem.at[0])]
    loads.append(pltpu.make_async_copy(near_hbm, hist_near, load_sem.at[1]))
    loads.append(pltpu.make_async_copy(src_hbm, src, load_sem.at[2]))
    for g in range(GROUPS):
        loads.append(
            pltpu.make_async_copy(vs_hbm.at[:, pl.ds(g * width, width)], v.at[g], load_sem.at[3 + g])
        )
    for place, origin in enumerate((me, left, right, across)):
        columns = pl.ds(pl.multiple_of(origin * rows, rows), rows)
        loads.append(
            pltpu.make_async_copy(
                z_hbm.at[:, columns], zr.at[:, pl.ds(place * rows, rows)], load_sem.at[3 + GROUPS + place]
            )
        )
    for load in loads:
        load.start()

    barrier = pltpu.get_barrier_semaphore()
    for neighbour in (left, right):
        pl.semaphore_signal(barrier, inc=1, device_id={"row": neighbour}, device_id_type=MESH)
    for d in range(1, subs):
        pl.semaphore_signal(barrier, inc=1, device_id={"sub": lax.rem(my_sub + d, subs)}, device_id_type=MESH)
    for d in range(1, zones):
        pl.semaphore_signal(barrier, inc=1, device_id={"zone": lax.rem(my_zone + d, zones)}, device_id_type=MESH)

    target = remote_sub[...].astype(F32)
    target_col = to_column(target, lines)
    same = target_col == target
    first, second = iota((lines, lines), 0), iota((lines, lines), 1)
    rank = jnp.sum(jnp.where(same & (first < second), 1.0, 0.0), axis=0, keepdims=True)
    rank_col = jnp.sum(jnp.where(same & (second < first), 1.0, 0.0), axis=1, keepdims=True)
    target_int = remote_sub[...]
    zone_of = target_int // subs
    sub_of = target_int - zone_of * subs
    slot_a = sub_of * block_a + zone_of * 2 + rank.astype(jnp.int32)
    slot_b = (target_col * 2.0 + rank_col).astype(jnp.int32)
    slots_out[...] = one_hot(iota((slots, lines), 0) == slot_a)
    slots_back[...] = one_hot(iota((lines, slots), 1) == slot_b)
    k = iota((slots, slots), 0)
    z_of, rest = k // (2 * subs), k - (k // (2 * subs)) * (2 * subs)
    swap[...] = one_hot(iota((slots, slots), 1) == (rest // 2) * block_a + z_of * 2 + (rest - (rest // 2) * 2))
    far_col = (to_column(far_node[...].astype(F32), lines) + 1.0).astype(jnp.int32)
    high = far_col // 16
    numbers = jnp.where(iota((lines, 128), 1) < 64, high, far_col - high * 16).astype(F32).astype(BF16)
    numbers_out = dot(slots_out[...], numbers).astype(BF16)

    def send_subs(out, got, which):
        got[pl.ds(my_sub, 1)] = out[pl.ds(my_sub, 1)]

        def one(d, carry):
            partner = lax.rem(my_sub + d, subs)
            pltpu.make_async_remote_copy(
                src_ref=out.at[partner],
                dst_ref=got.at[my_sub],
                send_sem=ex_send.at[which, 0],
                recv_sem=ex_recv.at[which, 0],
                device_id={"sub": partner},
                device_id_type=MESH,
            ).start()
            return carry

        lax.fori_loop(1, subs, one, 0)

    def send_zones(out, got, which):
        got[pl.ds(my_zone, 1)] = out[pl.ds(my_zone, 1)]

        def one(d, carry):
            partner = lax.rem(my_zone + d, zones)
            pltpu.make_async_remote_copy(
                src_ref=out.at[partner],
                dst_ref=got.at[my_zone],
                send_sem=ex_send.at[which, 1],
                recv_sem=ex_recv.at[which, 1],
                device_id={"zone": partner},
                device_id_type=MESH,
            ).start()
            return carry

        lax.fori_loop(1, zones, one, 0)

    def all_of(buffer, which, phase, axis, size):
        part = buffer.at[pl.ds(0, size - 1)]
        return pltpu.make_async_remote_copy(
            src_ref=part,
            dst_ref=part,
            send_sem=ex_send.at[which, phase],
            recv_sem=ex_recv.at[which, phase],
            device_id={axis: 0},
            device_id_type=MESH,
        )

    def wait_subs(buffer, which):
        all_of(buffer, which, 0, "sub", subs).wait_recv()

    def wait_zones(buffer, which):
        all_of(buffer, which, 1, "zone", zones).wait_recv()

    def turn(got):
        values = got.reshape(slots, got.shape[-1])
        return dot(swap[...], values).astype(BF16).reshape(zones, block_b, got.shape[-1])

    loads[0].wait()
    spread = slots_out[...]
    for step in range(2):
        values = dot(spread, hist_far[step].astype(BF16)).astype(BF16)
        if step == 0:
            oa0[:, :, :half] = values[:, :half].reshape(subs, block_a, half)
            oa0[:, :, half:] = numbers_out.reshape(subs, block_a, 128)
            oa1[...] = values[:, half:].reshape(subs, block_a, half)
        else:
            oa2[...] = values.reshape(subs, block_a, cases)
        if step == 0:
            pl.semaphore_wait(barrier, 2 + subs - 1 + zones - 1)
            send_subs(oa0, ra0, 0)
            send_subs(oa1, ra1, 1)
        else:
            send_subs(oa2, ra2, 2)

    near_row = near_node[...]
    near_col = to_column(near_row.astype(F32), lines).astype(jnp.int32)
    near_matrix = one_hot(iota((rows, lines), 0) == near_row)
    scatter[:, :lines] = near_matrix
    scatter[:, lines : 2 * lines] = near_matrix
    gather[:lines] = one_hot(iota((lines, rows), 1) == near_col)
    gain[...] = jnp.broadcast_to(to_column(line_gain[...], lines), (lines, width))
    on = switch_on[...].astype(F32) * switch_cond[...]
    eight = jnp.concatenate([on, jnp.zeros((8 - steps, rows), F32)], axis=0)
    columns = eight.T
    for step in range(steps):
        switched[step] = jnp.broadcast_to(columns[:, step : step + 1], (rows, width))
    for load in loads[1:]:
        load.wait()

    wait_subs(ra0, 0)
    ob0[...] = turn(ra0[...])
    send_zones(ob0, rb0, 0)
    wait_subs(ra1, 1)
    ob1[...] = turn(ra1[...])
    send_zones(ob1, rb1, 1)

    wait_zones(rb0, 0)
    arrived = rb0[:, :, half:].reshape(slots, 128)

    def node_of(numbers):
        numbers = numbers.astype(F32)
        return numbers[:, 0:1] * 16.0 + numbers[:, 64:65] - 1.0

    scatter[:, 2 * lines :] = one_hot(
        iota((rows, slots), 0) == to_row(node_of(arrived), slots).astype(jnp.int32)
    )
    gather[lines:] = one_hot(iota((slots, rows), 1) == node_of(dot(swap[...], arrived)).astype(jnp.int32))

    def set_near(history):
        top = history.astype(BF16)
        rhs[:lines] = top
        rhs[lines : 2 * lines] = (history - top.astype(F32)).astype(BF16)

    def inject(step, g, volts):
        at = pl.ds(pl.multiple_of(g * width, width), width)
        faulted = me * rows + iota((rows, width), 0) == fault_node[:, at]
        conduct = switched[step] + jnp.where(faulted, fault_cond[:, at], 0.0)
        lines_in = dot(scatter[...], rhs[...])
        x[step, g, :rows] = (src[step, :, at].astype(F32) + lines_in - conduct * volts).astype(BF16)
        for peer, place, sem in ((right, 1, left_sem), (left, 2, right_sem)):
            own_copy(step, g, peer, place, sem).start()

    def own_copy(step, g, peer, place, sem):
        return pltpu.make_async_remote_copy(
            src_ref=x.at[step, g, pl.ds(0, rows)],
            dst_ref=x.at[step, g, pl.ds(place * rows, rows)],
            send_sem=send_sem.at[step, g],
            recv_sem=sem.at[step, g],
            device_id={"row": peer},
            device_id_type=MESH,
        )

    def pass_on(step, g, peer, place, offset):
        return pltpu.make_async_remote_copy(
            src_ref=x.at[step, g, pl.ds(place * rows + offset, rows // 2)],
            dst_ref=x.at[step, g, pl.ds(3 * rows + offset, rows // 2)],
            send_sem=send_sem.at[step, g],
            recv_sem=far_sem.at[step, g],
            device_id={"row": peer},
            device_id_type=MESH,
        )

    def whole(step, g, count, sem):
        part = x.at[step, g, pl.ds(0, count * rows)]
        return pltpu.make_async_remote_copy(
            src_ref=part,
            dst_ref=part,
            send_sem=send_sem.at[step, g],
            recv_sem=sem.at[step, g],
            device_id={"row": right},
            device_id_type=MESH,
        )

    for g in range(GROUPS):
        if g == 2:
            wait_zones(rb1, 1)
        set_near(hist_near[0, :, g * width : (g + 1) * width])
        got = rb0 if g < 2 else rb1
        rhs[2 * lines :] = got[:, :, (g % 2) * width : (g % 2 + 1) * width].reshape(slots, width)
        inject(0, g, v[g])

    wait_subs(ra2, 2)
    ob2[...] = turn(ra2[...])
    send_zones(ob2, rb2, 2)

    def begin(item):
        step, g = item // GROUPS, lax.rem(item, GROUPS)
        whole(step, g, 1, left_sem).wait_recv()
        pass_on(step, g, right, 1, 0).start()
        whole(step, g, 1, right_sem).wait_recv()
        pass_on(step, g, left, 2, rows // 2).start()
        v[g] = dot(zr[:, : 3 * rows], x[step, g, : 3 * rows])

    def finish(item):
        step, g = item // GROUPS, lax.rem(item, GROUPS)
        pair, side = g // 2, lax.rem(g, 2)
        at = pl.ds(pl.multiple_of(g * width, width), width)
        in_half = pl.ds(pl.multiple_of(side * width, width), width)
        whole(step, g, 1, far_sem).wait_recv()
        v[g] += dot(zr[:, 3 * rows :], x[step, g, 3 * rows :])

        @pl.when(step == 0)
        def _():
            @pl.when(g == 0)
            def _():
                wait_zones(rb2, 2)

            set_near(hist_near[1, :, at])
            rhs[2 * lines :] = rb2[:, :, at].reshape(slots, width)

        @pl.when((step == 1) | (step == 2))
        def _():
            which = (step - 1) * 2 + pair

            @pl.when(side == 0)
            def _():
                wait_zones(rb.at[which], 3 + which)

            rhs[2 * lines :] = rb[which, :, :block_b, in_half].reshape(slots, width)
            returned = rb[which, :, block_b:, in_half].reshape(slots, width)
            set_near(gain[...] * dot(slots_back[...], returned) - hist_far[step - 1, :, at])

        @pl.when(step < steps - 1)
        def _():
            inject(step + 1, g, v[g])

        @pl.when(step == steps - 1)
        def _():
            pltpu.make_async_copy(v.at[g], out_hbm.at[:, at], out_sem.at[g]).start()

        @pl.when(step < 2)
        def _():
            which = step * 2 + pair
            volts = v[g]
            top = volts.astype(BF16)
            ends = dot(gather[...], top)
            near_volts = ends[:lines] + dot(gather[:lines], (volts - top.astype(F32)).astype(BF16))
            history = gain[...] * near_volts - hist_near[step, :, at]
            oa[which, :, :block_a, in_half] = (
                dot(slots_out[...], history.astype(BF16)).astype(BF16).reshape(subs, block_a, width)
            )
            oa[which, :, block_a:, in_half] = ends[lines:].astype(BF16).reshape(subs, block_a, width)

            @pl.when(side == 1)
            def _():
                send_subs(oa.at[which], ra.at[which], 3 + which)

        @pl.when((side == 0) & (item >= 2) & (item < 2 + 4 * 2))
        def _():
            which = item // 2 - 1
            wait_subs(ra.at[which], 3 + which)
            ob[which, :, :block_b] = turn(ra[which, :, :block_a])
            ob[which, :, block_b:] = turn(ra[which, :, block_a:])
            send_zones(ob.at[which], rb.at[which], 3 + which)

    for item in range(AHEAD):
        begin(item)

    def body(item, carry):
        @pl.when(item + AHEAD < items)
        def _():
            begin(item + AHEAD)

        finish(item)

        @pl.when(item >= GROUPS)
        def _():
            whole(item // GROUPS - 1, lax.rem(item, GROUPS), 3, far_sem).wait_send()

        return carry

    lax.fori_loop(0, items, body, 0)

    for g in range(GROUPS):
        whole(steps - 1, g, 3, far_sem).wait_send()
    for which, (sent_a, sent_b) in enumerate(((oa0, ob0), (oa1, ob1), (oa2, ob2))):
        all_of(sent_a, which, 0, "sub", subs).wait_send()
        all_of(sent_b, which, 1, "zone", zones).wait_send()
    for which in range(4):
        all_of(oa.at[which], 3 + which, 0, "sub", subs).wait_send()
        all_of(ob.at[which], 3 + which, 1, "zone", zones).wait_send()
    for g in range(GROUPS):
        at = pl.ds(g * width, width)
        pltpu.make_async_copy(v.at[g], out_hbm.at[:, at], out_sem.at[g]).wait()


def local(zones, subs, *arguments):
    (
        z_inverse,
        sources,
        v_start,
        hist_near,
        hist_far,
        switch_on,
        switch_cond,
        fault_node,
        fault_cond,
        remote_sub,
        near_node,
        far_node,
        line_gain,
    ) = arguments
    steps, _, rows, cases = sources.shape
    lines = near_node.shape[1]
    slots = 2 * zones * subs
    block_a, block_b = 2 * zones, 2 * subs
    width = cases // GROUPS
    half = 2 * width

    def exchange(wide, tall=1, count=None):
        lead = () if count is None else (count,)
        return [
            pltpu.VMEM(lead + (subs, tall * block_a, wide), BF16),
            pltpu.VMEM(lead + (subs, tall * block_a, wide), BF16),
            pltpu.VMEM(lead + (zones, tall * block_b, wide), BF16),
            pltpu.VMEM(lead + (zones, tall * block_b, wide), BF16),
        ]

    hbm = pl.BlockSpec(memory_space=pl.ANY)
    vmem = pl.BlockSpec(memory_space=pltpu.VMEM)
    result = pl.pallas_call(
        functools.partial(kernel, zones, subs),
        out_shape=jax.ShapeDtypeStruct((rows, cases), F32),
        in_specs=[hbm] * 5 + [vmem] * 8,
        out_specs=hbm,
        scratch_shapes=[
            pltpu.VMEM((rows, 4 * rows), BF16),
            pltpu.VMEM((steps, GROUPS, 4 * rows, width), BF16),
            pltpu.VMEM((GROUPS, rows, width), F32),
            pltpu.VMEM((steps, rows, cases), BF16),
            pltpu.VMEM((2, lines, cases), F32),
            pltpu.VMEM((2, lines, cases), F32),
            pltpu.VMEM((steps, rows, width), F32),
            pltpu.VMEM((rows, 2 * lines + slots), BF16),
            pltpu.VMEM((lines + slots, rows), BF16),
            pltpu.VMEM((slots, lines), BF16),
            pltpu.VMEM((lines, slots), BF16),
            pltpu.VMEM((slots, slots), BF16),
            pltpu.VMEM((lines, width), F32),
            pltpu.VMEM((2 * lines + slots, width), BF16),
            *exchange(half + 128),
            *exchange(half),
            *exchange(cases),
            *exchange(half, 2, 4),
            pltpu.SemaphoreType.DMA((3 + GROUPS + 4,)),
            pltpu.SemaphoreType.DMA((steps, GROUPS)),
            pltpu.SemaphoreType.DMA((steps, GROUPS)),
            pltpu.SemaphoreType.DMA((steps, GROUPS)),
            pltpu.SemaphoreType.DMA((steps, GROUPS)),
            pltpu.SemaphoreType.DMA((7, 2)),
            pltpu.SemaphoreType.DMA((7, 2)),
            pltpu.SemaphoreType.DMA((GROUPS,)),
        ],
        compiler_params=pltpu.CompilerParams(
            collective_id=0, has_side_effects=True, vmem_limit_bytes=40 * 1024 * 1024
        ),
    )(
        z_inverse[0],
        sources[:, 0],
        v_start[0],
        hist_near[:, 0],
        hist_far[:, 0],
        switch_on[:, 0],
        switch_cond,
        fault_node[None],
        fault_cond[None],
        remote_sub[:, :, 0],
        near_node,
        far_node,
        line_gain,
    )
    return result[None]


def solution(mesh):
    placed = (
        P(("zone", "sub"), "row", None),
        P(None, ("zone", "sub"), "row", None),
        P(("zone", "sub"), "row", None),
        P(None, ("zone", "sub"), "row", None),
        P(None, ("zone", "sub"), "row", None),
        P(None, ("zone", "sub"), "row"),
        P(("zone", "sub"), "row"),
        P(),
        P(),
        P(("zone", "sub"), "row", None),
        P(("zone", "sub"), "row"),
        P(("zone", "sub"), "row"),
        P(("zone", "sub"), "row"),
    )
    return jax.shard_map(
        functools.partial(local, mesh.shape["zone"], mesh.shape["sub"]),
        mesh=mesh,
        in_specs=placed,
        out_specs=P(("zone", "sub"), "row", None),
        check_vma=False,
    )
```

```python
import functools

import jax
import jax.numpy as jnp
from jax import lax
from jax.experimental import pallas as pl
from jax.experimental.pallas import tpu as pltpu
from jax.sharding import PartitionSpec as P

MESH = pl.DeviceIdType.MESH
F32 = jnp.float32
BF16 = jnp.bfloat16
GROUPS = 4
AHEAD = 2


def dot(a, b):
    return jnp.dot(a, b, preferred_element_type=F32)


def iota(shape, dim):
    return lax.broadcasted_iota(jnp.int32, shape, dim)


def one_hot(mask):
    return jnp.where(mask, 1.0, 0.0).astype(BF16)


def to_column(row, size):
    eye = iota((size, size), 0) == iota((size, size), 1)
    return jnp.sum(jnp.where(eye, row, 0.0), axis=1, keepdims=True)


def to_row(column, size):
    eye = iota((size, size), 0) == iota((size, size), 1)
    return jnp.sum(jnp.where(eye, column, 0.0), axis=0, keepdims=True)


def kernel(
    zones,
    subs,
    z_hbm,
    src_hbm,
    vs_hbm,
    near_hbm,
    far_hbm,
    *rest,
):
    small_hbm, out_hbm, small, rest = rest[:8], rest[8], rest[9:17], rest[17:]
    (
        switch_on,
        switch_cond,
        fault_node,
        fault_cond,
        remote_sub,
        near_node,
        far_node,
        line_gain,
    ) = small
    (
        zr,
        x,
        v,
        src,
        hist_near,
        hist_far,
        switched,
        scatter,
        gather,
        slots_out,
        slots_back,
        swap,
        gain,
        rhs,
        oa0,
        ra0,
        ob0,
        rb0,
        oa1,
        ra1,
        ob1,
        rb1,
        oa2,
        ra2,
        ob2,
        rb2,
        oa,
        ra,
        ob,
        rb,
        load_sem,
        send_sem,
        left_sem,
        right_sem,
        far_sem,
        ex_send,
        ex_recv,
        out_sem,
    ) = rest
    rows, nodes = z_hbm.shape
    steps, _, cases = src_hbm.shape
    lines = near_node.shape[1]
    slots = 2 * zones * subs
    block_a, block_b = 2 * zones, 2 * subs
    width = cases // GROUPS
    half = 2 * width
    items = steps * GROUPS
    my_zone, my_sub, me = (lax.axis_index(name) for name in ("zone", "sub", "row"))
    right, left, across = lax.rem(me + 1, 4), lax.rem(me + 3, 4), lax.rem(me + 2, 4)

    loads = [
        pltpu.make_async_copy(there, here, load_sem.at[3 + GROUPS + 4 + number])
        for number, (there, here) in enumerate(zip(small_hbm, small))
    ]
    loads.append(pltpu.make_async_copy(far_hbm, hist_far, load_sem.at[0]))
    loads.append(pltpu.make_async_copy(near_hbm, hist_near, load_sem.at[1]))
    loads.append(pltpu.make_async_copy(src_hbm, src, load_sem.at[2]))
    for g in range(GROUPS):
        loads.append(
            pltpu.make_async_copy(vs_hbm.at[:, pl.ds(g * width, width)], v.at[g], load_sem.at[3 + g])
        )
    for place, origin in enumerate((me, left, right, across)):
        columns = pl.ds(pl.multiple_of(origin * rows, rows), rows)
        loads.append(
            pltpu.make_async_copy(
                z_hbm.at[:, columns], zr.at[:, pl.ds(place * rows, rows)], load_sem.at[3 + GROUPS + place]
            )
        )
    for load in loads:
        load.start()

    barrier = pltpu.get_barrier_semaphore()
    for neighbour in (left, right):
        pl.semaphore_signal(barrier, inc=1, device_id={"row": neighbour}, device_id_type=MESH)
    for d in range(1, subs):
        pl.semaphore_signal(barrier, inc=1, device_id={"sub": lax.rem(my_sub + d, subs)}, device_id_type=MESH)
    for d in range(1, zones):
        pl.semaphore_signal(barrier, inc=1, device_id={"zone": lax.rem(my_zone + d, zones)}, device_id_type=MESH)

    for load in loads[:8]:
        load.wait()

    target = remote_sub[...].astype(F32)
    target_col = to_column(target, lines)
    same = target_col == target
    first, second = iota((lines, lines), 0), iota((lines, lines), 1)
    rank = jnp.sum(jnp.where(same & (first < second), 1.0, 0.0), axis=0, keepdims=True)
    rank_col = jnp.sum(jnp.where(same & (second < first), 1.0, 0.0), axis=1, keepdims=True)
    target_int = remote_sub[...]
    zone_of = target_int // subs
    sub_of = target_int - zone_of * subs
    slot_a = sub_of * block_a + zone_of * 2 + rank.astype(jnp.int32)
    slot_b = (target_col * 2.0 + rank_col).astype(jnp.int32)
    slots_out[...] = one_hot(iota((slots, lines), 0) == slot_a)
    slots_back[...] = one_hot(iota((lines, slots), 1) == slot_b)
    k = iota((slots, slots), 0)
    z_of, rest = k // (2 * subs), k - (k // (2 * subs)) * (2 * subs)
    swap[...] = one_hot(iota((slots, slots), 1) == (rest // 2) * block_a + z_of * 2 + (rest - (rest // 2) * 2))
    far_col = (to_column(far_node[...].astype(F32), lines) + 1.0).astype(jnp.int32)
    high = far_col // 16
    numbers = jnp.where(iota((lines, 128), 1) < 64, high, far_col - high * 16).astype(F32).astype(BF16)
    numbers_out = dot(slots_out[...], numbers).astype(BF16)

    def send_subs(out, got, which):
        got[pl.ds(my_sub, 1)] = out[pl.ds(my_sub, 1)]

        def one(d, carry):
            partner = lax.rem(my_sub + d, subs)
            pltpu.make_async_remote_copy(
                src_ref=out.at[partner],
                dst_ref=got.at[my_sub],
                send_sem=ex_send.at[which, 0],
                recv_sem=ex_recv.at[which, 0],
                device_id={"sub": partner},
                device_id_type=MESH,
            ).start()
            return carry

        lax.fori_loop(1, subs, one, 0)

    def send_zones(out, got, which):
        got[pl.ds(my_zone, 1)] = out[pl.ds(my_zone, 1)]

        def one(d, carry):
            partner = lax.rem(my_zone + d, zones)
            pltpu.make_async_remote_copy(
                src_ref=out.at[partner],
                dst_ref=got.at[my_zone],
                send_sem=ex_send.at[which, 1],
                recv_sem=ex_recv.at[which, 1],
                device_id={"zone": partner},
                device_id_type=MESH,
            ).start()
            return carry

        lax.fori_loop(1, zones, one, 0)

    def all_of(buffer, which, phase, axis, size):
        part = buffer.at[pl.ds(0, size - 1)]
        return pltpu.make_async_remote_copy(
            src_ref=part,
            dst_ref=part,
            send_sem=ex_send.at[which, phase],
            recv_sem=ex_recv.at[which, phase],
            device_id={axis: 0},
            device_id_type=MESH,
        )

    def wait_subs(buffer, which):
        all_of(buffer, which, 0, "sub", subs).wait_recv()

    def wait_zones(buffer, which):
        all_of(buffer, which, 1, "zone", zones).wait_recv()

    def turn(got):
        values = got.reshape(slots, got.shape[-1])
        return dot(swap[...], values).astype(BF16).reshape(zones, block_b, got.shape[-1])

    loads[8].wait()
    spread = slots_out[...]
    for step in range(2):
        values = dot(spread, hist_far[step].astype(BF16)).astype(BF16)
        if step == 0:
            oa0[:, :, :half] = values[:, :half].reshape(subs, block_a, half)
            oa0[:, :, half:] = numbers_out.reshape(subs, block_a, 128)
            oa1[...] = values[:, half:].reshape(subs, block_a, half)
        else:
            oa2[...] = values.reshape(subs, block_a, cases)
        if step == 0:
            pl.semaphore_wait(barrier, 2 + subs - 1 + zones - 1)
            send_subs(oa0, ra0, 0)
            send_subs(oa1, ra1, 1)
        else:
            send_subs(oa2, ra2, 2)

    near_row = near_node[...]
    near_col = to_column(near_row.astype(F32), lines).astype(jnp.int32)
    near_matrix = one_hot(iota((rows, lines), 0) == near_row)
    scatter[:, :lines] = near_matrix
    scatter[:, lines : 2 * lines] = near_matrix
    gather[:lines] = one_hot(iota((lines, rows), 1) == near_col)
    gain[...] = jnp.broadcast_to(to_column(line_gain[...], lines), (lines, width))
    on = switch_on[:, 0].astype(F32) * switch_cond[...]
    eight = jnp.concatenate([on, jnp.zeros((8 - steps, rows), F32)], axis=0)
    columns = eight.T
    for step in range(steps):
        switched[step] = jnp.broadcast_to(columns[:, step : step + 1], (rows, width))
    for load in loads[9:]:
        load.wait()

    wait_subs(ra0, 0)
    ob0[...] = turn(ra0[...])
    send_zones(ob0, rb0, 0)
    wait_subs(ra1, 1)
    ob1[...] = turn(ra1[...])
    send_zones(ob1, rb1, 1)

    wait_zones(rb0, 0)
    arrived = rb0[:, :, half:].reshape(slots, 128)

    def node_of(numbers):
        numbers = numbers.astype(F32)
        return numbers[:, 0:1] * 16.0 + numbers[:, 64:65] - 1.0

    scatter[:, 2 * lines :] = one_hot(
        iota((rows, slots), 0) == to_row(node_of(arrived), slots).astype(jnp.int32)
    )
    gather[lines:] = one_hot(iota((slots, rows), 1) == node_of(dot(swap[...], arrived)).astype(jnp.int32))

    def set_near(history):
        top = history.astype(BF16)
        rhs[:lines] = top
        rhs[lines : 2 * lines] = (history - top.astype(F32)).astype(BF16)

    def inject(step, g, volts):
        at = pl.ds(pl.multiple_of(g * width, width), width)
        faulted = me * rows + iota((rows, width), 0) == fault_node[:, at]
        conduct = switched[step] + jnp.where(faulted, fault_cond[:, at], 0.0)
        lines_in = dot(scatter[...], rhs[...])
        x[step, g, :rows] = (src[step, :, at].astype(F32) + lines_in - conduct * volts).astype(BF16)
        for peer, place, sem in ((right, 1, left_sem), (left, 2, right_sem)):
            own_copy(step, g, peer, place, sem).start()

    def own_copy(step, g, peer, place, sem):
        return pltpu.make_async_remote_copy(
            src_ref=x.at[step, g, pl.ds(0, rows)],
            dst_ref=x.at[step, g, pl.ds(place * rows, rows)],
            send_sem=send_sem.at[step, g],
            recv_sem=sem.at[step, g],
            device_id={"row": peer},
            device_id_type=MESH,
        )

    def pass_on(step, g, peer, place, offset):
        return pltpu.make_async_remote_copy(
            src_ref=x.at[step, g, pl.ds(place * rows + offset, rows // 2)],
            dst_ref=x.at[step, g, pl.ds(3 * rows + offset, rows // 2)],
            send_sem=send_sem.at[step, g],
            recv_sem=far_sem.at[step, g],
            device_id={"row": peer},
            device_id_type=MESH,
        )

    def whole(step, g, count, sem):
        part = x.at[step, g, pl.ds(0, count * rows)]
        return pltpu.make_async_remote_copy(
            src_ref=part,
            dst_ref=part,
            send_sem=send_sem.at[step, g],
            recv_sem=sem.at[step, g],
            device_id={"row": right},
            device_id_type=MESH,
        )

    for g in range(GROUPS):
        if g == 2:
            wait_zones(rb1, 1)
        set_near(hist_near[0, :, g * width : (g + 1) * width])
        got = rb0 if g < 2 else rb1
        rhs[2 * lines :] = got[:, :, (g % 2) * width : (g % 2 + 1) * width].reshape(slots, width)
        inject(0, g, v[g])

    wait_subs(ra2, 2)
    ob2[...] = turn(ra2[...])
    send_zones(ob2, rb2, 2)

    def begin(item):
        step, g = item // GROUPS, lax.rem(item, GROUPS)
        whole(step, g, 1, left_sem).wait_recv()
        pass_on(step, g, right, 1, 0).start()
        whole(step, g, 1, right_sem).wait_recv()
        pass_on(step, g, left, 2, rows // 2).start()
        v[g] = dot(zr[:, : 3 * rows], x[step, g, : 3 * rows])

    def finish(item):
        step, g = item // GROUPS, lax.rem(item, GROUPS)
        pair, side = g // 2, lax.rem(g, 2)
        at = pl.ds(pl.multiple_of(g * width, width), width)
        in_half = pl.ds(pl.multiple_of(side * width, width), width)
        whole(step, g, 1, far_sem).wait_recv()
        v[g] += dot(zr[:, 3 * rows :], x[step, g, 3 * rows :])

        @pl.when(step == 0)
        def _():
            @pl.when(g == 0)
            def _():
                wait_zones(rb2, 2)

            set_near(hist_near[1, :, at])
            rhs[2 * lines :] = rb2[:, :, at].reshape(slots, width)

        @pl.when((step == 1) | (step == 2))
        def _():
            which = (step - 1) * 2 + pair

            @pl.when(side == 0)
            def _():
                wait_zones(rb.at[which], 3 + which)

            rhs[2 * lines :] = rb[which, :, :block_b, in_half].reshape(slots, width)
            returned = rb[which, :, block_b:, in_half].reshape(slots, width)
            set_near(gain[...] * dot(slots_back[...], returned) - hist_far[step - 1, :, at])

        @pl.when(step < steps - 1)
        def _():
            inject(step + 1, g, v[g])

        @pl.when(step == steps - 1)
        def _():
            pltpu.make_async_copy(v.at[g], out_hbm.at[:, at], out_sem.at[g]).start()

        @pl.when(step < 2)
        def _():
            which = step * 2 + pair
            volts = v[g]
            top = volts.astype(BF16)
            ends = dot(gather[...], top)
            near_volts = ends[:lines] + dot(gather[:lines], (volts - top.astype(F32)).astype(BF16))
            history = gain[...] * near_volts - hist_near[step, :, at]
            oa[which, :, :block_a, in_half] = (
                dot(slots_out[...], history.astype(BF16)).astype(BF16).reshape(subs, block_a, width)
            )
            oa[which, :, block_a:, in_half] = ends[lines:].astype(BF16).reshape(subs, block_a, width)

            @pl.when(side == 1)
            def _():
                send_subs(oa.at[which], ra.at[which], 3 + which)

        @pl.when((side == 0) & (item >= 2) & (item < 2 + 4 * 2))
        def _():
            which = item // 2 - 1
            wait_subs(ra.at[which], 3 + which)
            ob[which, :, :block_b] = turn(ra[which, :, :block_a])
            ob[which, :, block_b:] = turn(ra[which, :, block_a:])
            send_zones(ob.at[which], rb.at[which], 3 + which)

    for item in range(AHEAD):
        begin(item)

    def body(item, carry):
        @pl.when(item + AHEAD < items)
        def _():
            begin(item + AHEAD)

        finish(item)

        @pl.when(item >= GROUPS)
        def _():
            whole(item // GROUPS - 1, lax.rem(item, GROUPS), 3, far_sem).wait_send()

        return carry

    lax.fori_loop(0, items, body, 0)

    for g in range(GROUPS):
        whole(steps - 1, g, 3, far_sem).wait_send()
    for which, (sent_a, sent_b) in enumerate(((oa0, ob0), (oa1, ob1), (oa2, ob2))):
        all_of(sent_a, which, 0, "sub", subs).wait_send()
        all_of(sent_b, which, 1, "zone", zones).wait_send()
    for which in range(4):
        all_of(oa.at[which], 3 + which, 0, "sub", subs).wait_send()
        all_of(ob.at[which], 3 + which, 1, "zone", zones).wait_send()
    for g in range(GROUPS):
        at = pl.ds(g * width, width)
        pltpu.make_async_copy(v.at[g], out_hbm.at[:, at], out_sem.at[g]).wait()


def local(zones, subs, *arguments):
    (
        z_inverse,
        sources,
        v_start,
        hist_near,
        hist_far,
        switch_on,
        switch_cond,
        fault_node,
        fault_cond,
        remote_sub,
        near_node,
        far_node,
        line_gain,
    ) = arguments
    steps, _, rows, cases = sources.shape
    lines = near_node.shape[1]
    slots = 2 * zones * subs
    block_a, block_b = 2 * zones, 2 * subs
    width = cases // GROUPS
    half = 2 * width

    def exchange(wide, tall=1, count=None):
        lead = () if count is None else (count,)
        return [
            pltpu.VMEM(lead + (subs, tall * block_a, wide), BF16),
            pltpu.VMEM(lead + (subs, tall * block_a, wide), BF16),
            pltpu.VMEM(lead + (zones, tall * block_b, wide), BF16),
            pltpu.VMEM(lead + (zones, tall * block_b, wide), BF16),
        ]

    hbm = pl.BlockSpec(memory_space=pltpu.HBM)
    small = (
        switch_on,
        switch_cond,
        fault_node[None],
        fault_cond[None],
        remote_sub[:, :, 0],
        near_node,
        far_node,
        line_gain,
    )
    result = pl.pallas_call(
        functools.partial(kernel, zones, subs),
        out_shape=jax.ShapeDtypeStruct((rows, cases), F32),
        in_specs=[hbm] * (5 + len(small)),
        out_specs=hbm,
        scratch_shapes=[
            *(pltpu.VMEM(array.shape, array.dtype) for array in small),
            pltpu.VMEM((rows, 4 * rows), BF16),
            pltpu.VMEM((steps, GROUPS, 4 * rows, width), BF16),
            pltpu.VMEM((GROUPS, rows, width), F32),
            pltpu.VMEM((steps, rows, cases), BF16),
            pltpu.VMEM((2, lines, cases), F32),
            pltpu.VMEM((2, lines, cases), F32),
            pltpu.VMEM((steps, rows, width), F32),
            pltpu.VMEM((rows, 2 * lines + slots), BF16),
            pltpu.VMEM((lines + slots, rows), BF16),
            pltpu.VMEM((slots, lines), BF16),
            pltpu.VMEM((lines, slots), BF16),
            pltpu.VMEM((slots, slots), BF16),
            pltpu.VMEM((lines, width), F32),
            pltpu.VMEM((2 * lines + slots, width), BF16),
            *exchange(half + 128),
            *exchange(half),
            *exchange(cases),
            *exchange(half, 2, 4),
            pltpu.SemaphoreType.DMA((3 + GROUPS + 4 + 8,)),
            pltpu.SemaphoreType.DMA((steps, GROUPS)),
            pltpu.SemaphoreType.DMA((steps, GROUPS)),
            pltpu.SemaphoreType.DMA((steps, GROUPS)),
            pltpu.SemaphoreType.DMA((steps, GROUPS)),
            pltpu.SemaphoreType.DMA((7, 2)),
            pltpu.SemaphoreType.DMA((7, 2)),
            pltpu.SemaphoreType.DMA((GROUPS,)),
        ],
        compiler_params=pltpu.CompilerParams(
            collective_id=0, has_side_effects=True, vmem_limit_bytes=56 * 1024 * 1024
        ),
    )(
        z_inverse[0],
        sources[:, 0],
        v_start[0],
        hist_near[:, 0],
        hist_far[:, 0],
        *small,
    )
    return result[None]


def solution(mesh):
    placed = (
        P(("zone", "sub"), "row", None),
        P(None, ("zone", "sub"), "row", None),
        P(("zone", "sub"), "row", None),
        P(None, ("zone", "sub"), "row", None),
        P(None, ("zone", "sub"), "row", None),
        P(None, ("zone", "sub"), "row"),
        P(("zone", "sub"), "row"),
        P(),
        P(),
        P(("zone", "sub"), "row", None),
        P(("zone", "sub"), "row"),
        P(("zone", "sub"), "row"),
        P(("zone", "sub"), "row"),
    )
    return jax.shard_map(
        functools.partial(local, mesh.shape["zone"], mesh.shape["sub"]),
        mesh=mesh,
        in_specs=placed,
        out_specs=P(("zone", "sub"), "row", None),
        check_vma=False,
    )
```

```python
import functools

import jax
import jax.numpy as jnp
from jax import lax
from jax.experimental import pallas as pl
from jax.experimental.pallas import tpu as pltpu
from jax.sharding import PartitionSpec as P

MESH = pl.DeviceIdType.MESH
F32 = jnp.float32
BF16 = jnp.bfloat16
GROUPS = 4
EARLY = 2
AHEAD = 2


def dot(a, b):
    return jnp.dot(a, b, preferred_element_type=F32)


def iota(shape, dim):
    return lax.broadcasted_iota(jnp.int32, shape, dim)


def one_hot(mask):
    return jnp.where(mask, 1.0, 0.0).astype(BF16)


def to_column(row, size):
    eye = iota((size, size), 0) == iota((size, size), 1)
    return jnp.sum(jnp.where(eye, row, 0.0), axis=1, keepdims=True)


def to_row(column, size):
    eye = iota((size, size), 0) == iota((size, size), 1)
    return jnp.sum(jnp.where(eye, column, 0.0), axis=0, keepdims=True)


def kernel(
    zones,
    subs,
    z_hbm,
    src_hbm,
    vs_hbm,
    near_hbm,
    far_hbm,
    *rest,
):
    small_hbm, out_hbm, small, rest = rest[:8], rest[8], rest[9:17], rest[17:]
    (
        switch_on,
        switch_cond,
        fault_node,
        fault_cond,
        remote_sub,
        near_node,
        far_node,
        line_gain,
    ) = small
    (
        zr,
        x,
        v,
        src,
        hist_near,
        hist_far,
        switched,
        scatter,
        gather,
        slots_out,
        slots_back,
        swap,
        gain,
        rhs,
        oa0,
        ra0,
        ob0,
        rb0,
        oa1,
        ra1,
        ob1,
        rb1,
        oa2,
        ra2,
        ob2,
        rb2,
        oa,
        ra,
        ob,
        rb,
        late_lines,
        selected,
        fix_send,
        fix_recv,
        load_sem,
        send_sem,
        left_sem,
        right_sem,
        far_sem,
        ex_send,
        ex_recv,
        out_sem,
    ) = rest
    rows, nodes = z_hbm.shape
    steps, _, cases = src_hbm.shape
    lines = near_node.shape[1]
    slots = 2 * zones * subs
    block_a, block_b = 2 * subs, 2 * zones
    width = cases // GROUPS
    half = 2 * width
    early, late = EARLY * width, (GROUPS - EARLY) * width
    items = steps * GROUPS
    my_zone, my_sub, me = (lax.axis_index(name) for name in ("zone", "sub", "row"))
    right, left, across = lax.rem(me + 1, 4), lax.rem(me + 3, 4), lax.rem(me + 2, 4)

    loads = [
        pltpu.make_async_copy(there, here, load_sem.at[3 + GROUPS + 4 + number])
        for number, (there, here) in enumerate(zip(small_hbm, small))
    ]
    loads.append(pltpu.make_async_copy(far_hbm, hist_far, load_sem.at[0]))
    loads.append(pltpu.make_async_copy(near_hbm, hist_near, load_sem.at[1]))
    loads.append(pltpu.make_async_copy(src_hbm, src, load_sem.at[2]))
    for g in range(GROUPS):
        loads.append(
            pltpu.make_async_copy(vs_hbm.at[:, pl.ds(g * width, width)], v.at[g], load_sem.at[3 + g])
        )
    for place, origin in enumerate((me, left, right, across)):
        columns = pl.ds(pl.multiple_of(origin * rows, rows), rows)
        loads.append(
            pltpu.make_async_copy(
                z_hbm.at[:, columns], zr.at[:, pl.ds(place * rows, rows)], load_sem.at[3 + GROUPS + place]
            )
        )
    for load in loads:
        load.start()

    barrier = pltpu.get_barrier_semaphore()
    for neighbour in (left, right):
        pl.semaphore_signal(barrier, inc=1, device_id={"row": neighbour}, device_id_type=MESH)
    for d in range(1, subs):
        pl.semaphore_signal(barrier, inc=1, device_id={"sub": lax.rem(my_sub + d, subs)}, device_id_type=MESH)
    for d in range(1, zones):
        pl.semaphore_signal(barrier, inc=1, device_id={"zone": lax.rem(my_zone + d, zones)}, device_id_type=MESH)

    for load in loads[:8]:
        load.wait()

    target = remote_sub[...].astype(F32)
    target_col = to_column(target, lines)
    same = target_col == target
    first, second = iota((lines, lines), 0), iota((lines, lines), 1)
    rank = jnp.sum(jnp.where(same & (first < second), 1.0, 0.0), axis=0, keepdims=True)
    rank_col = jnp.sum(jnp.where(same & (second < first), 1.0, 0.0), axis=1, keepdims=True)
    target_int = remote_sub[...]
    slot_a = target_int * 2 + rank.astype(jnp.int32)
    zone_col = target_col.astype(jnp.int32) // subs
    sub_col = target_col.astype(jnp.int32) - zone_col * subs
    slot_b = sub_col * block_b + zone_col * 2 + rank_col.astype(jnp.int32)
    slots_out[...] = one_hot(iota((slots, lines), 0) == slot_a)
    slots_back[...] = one_hot(iota((lines, slots), 1) == slot_b)
    k = iota((slots, slots), 0)
    sub_of, rest = k // block_b, k - (k // block_b) * block_b
    swap[...] = one_hot(iota((slots, slots), 1) == (rest // 2) * block_a + sub_of * 2 + (rest - (rest // 2) * 2))
    far_col = (to_column(far_node[...].astype(F32), lines) + 1.0).astype(jnp.int32)
    high = far_col // 16
    numbers = jnp.where(iota((lines, 128), 1) < 64, high, far_col - high * 16).astype(F32).astype(BF16)
    numbers_out = dot(slots_out[...], numbers).astype(BF16)

    hops = (("zone", my_zone, zones), ("sub", my_sub, subs))

    def send_hop(phase, out, got, which):
        axis, my, size = hops[phase]
        got[pl.ds(my, 1)] = out[pl.ds(my, 1)]

        def one(d, carry):
            partner = lax.rem(my + d, size)
            pltpu.make_async_remote_copy(
                src_ref=out.at[partner],
                dst_ref=got.at[my],
                send_sem=ex_send.at[which, phase],
                recv_sem=ex_recv.at[which, phase],
                device_id={axis: partner},
                device_id_type=MESH,
            ).start()
            return carry

        lax.fori_loop(1, size, one, 0)

    def all_of(phase, buffer, which):
        axis, my, size = hops[phase]
        part = buffer.at[pl.ds(0, size - 1)]
        return pltpu.make_async_remote_copy(
            src_ref=part,
            dst_ref=part,
            send_sem=ex_send.at[which, phase],
            recv_sem=ex_recv.at[which, phase],
            device_id={axis: lax.rem(my + 1, size)},
            device_id_type=MESH,
        )

    def turn(got):
        values = got.reshape(slots, got.shape[-1])
        return dot(swap[...], values).astype(BF16).reshape(subs, block_b, got.shape[-1])

    near_row = near_node[...]
    near_col = to_column(near_row.astype(F32), lines).astype(jnp.int32)
    near_matrix = one_hot(iota((rows, lines), 0) == near_row)
    scatter[:, :lines] = near_matrix
    scatter[:, lines : 2 * lines] = near_matrix
    gather[:lines] = one_hot(iota((lines, rows), 1) == near_col)
    gain[...] = jnp.broadcast_to(to_column(line_gain[...], lines), (lines, width))
    on = switch_on[:, 0].astype(F32) * switch_cond[...]
    eight = jnp.concatenate([on, jnp.zeros((8 - steps, rows), F32)], axis=0)
    columns = eight.T
    for step in range(steps):
        switched[step] = jnp.broadcast_to(columns[:, step : step + 1], (rows, width))

    loads[8].wait()
    spread = slots_out[...]
    values = dot(spread, hist_far[0].astype(BF16)).astype(BF16)
    oa0[:, :, :early] = values[:, :early].reshape(zones, block_a, early)
    oa0[:, :, early:] = numbers_out.reshape(zones, block_a, 128)
    oa1[...] = values[:, early:].reshape(zones, block_a, late)
    oa2[...] = dot(spread, hist_far[1].astype(BF16)).astype(BF16).reshape(zones, block_a, cases)

    def set_near(history):
        top = history.astype(BF16)
        rhs[:lines] = top
        rhs[lines : 2 * lines] = (history - top.astype(F32)).astype(BF16)

    def inject(step, g, volts, lines_in):
        at = pl.ds(pl.multiple_of(g * width, width), width)
        faulted = me * rows + iota((rows, width), 0) == fault_node[:, at]
        conduct = switched[step] + jnp.where(faulted, fault_cond[:, at], 0.0)
        x[step, g, :rows] = (src[step, :, at].astype(F32) + lines_in - conduct * volts).astype(BF16)

    def send_own(step, g):
        for peer, place, sem in ((right, 1, left_sem), (left, 2, right_sem)):
            own_copy(step, g, peer, place, sem).start()

    def own_copy(step, g, peer, place, sem):
        return pltpu.make_async_remote_copy(
            src_ref=x.at[step, g, pl.ds(0, rows)],
            dst_ref=x.at[step, g, pl.ds(place * rows, rows)],
            send_sem=send_sem.at[step, g],
            recv_sem=sem.at[step, g],
            device_id={"row": peer},
            device_id_type=MESH,
        )

    def pass_on(step, g, peer, place, offset):
        return pltpu.make_async_remote_copy(
            src_ref=x.at[step, g, pl.ds(place * rows + offset, rows // 2)],
            dst_ref=x.at[step, g, pl.ds(3 * rows + offset, rows // 2)],
            send_sem=send_sem.at[step, g],
            recv_sem=far_sem.at[step, g],
            device_id={"row": peer},
            device_id_type=MESH,
        )

    def whole(step, g, count, sem):
        part = x.at[step, g, pl.ds(0, count * rows)]
        return pltpu.make_async_remote_copy(
            src_ref=part,
            dst_ref=part,
            send_sem=send_sem.at[step, g],
            recv_sem=sem.at[step, g],
            device_id={"row": right},
            device_id_type=MESH,
        )

    def begin(item):
        step, g = item // GROUPS, lax.rem(item, GROUPS)
        whole(step, g, 1, left_sem).wait_recv()
        pass_on(step, g, right, 1, 0).start()
        whole(step, g, 1, right_sem).wait_recv()
        pass_on(step, g, left, 2, rows // 2).start()

    def correct(peer, place, sem):
        return pltpu.make_async_remote_copy(
            src_ref=late_lines.at[0],
            dst_ref=late_lines.at[place],
            send_sem=fix_send.at[place - 1],
            recv_sem=sem,
            device_id={"row": peer},
            device_id_type=MESH,
        )

    def correct_on(peer, place, offset):
        return pltpu.make_async_remote_copy(
            src_ref=late_lines.at[place, pl.ds(offset, slots // 2)],
            dst_ref=late_lines.at[3, pl.ds(offset, slots // 2)],
            send_sem=fix_send.at[place + 1],
            recv_sem=fix_recv.at[place + 1],
            device_id={"row": peer},
            device_id_type=MESH,
        )

    corrections = (correct(right, 1, fix_recv.at[0]), correct(left, 2, fix_recv.at[1]))
    corrections_on = (correct_on(right, 1, 0), correct_on(left, 2, slots // 2))

    for load in loads[9:]:
        load.wait()
    for g in range(EARLY):
        set_near(hist_near[0, :, g * width : (g + 1) * width])
        inject(0, g, v[g], dot(scatter[:, : 2 * lines], rhs[: 2 * lines]))
    pl.semaphore_wait(barrier, 2 + subs - 1 + zones - 1)
    send_hop(0, oa0, ra0, 0)
    for g in range(2):
        send_own(0, g)
    send_hop(0, oa1, ra1, 1)
    send_hop(0, oa2, ra2, 2)
    for which, (got, out, last) in enumerate(((ra0, ob0, rb0), (ra1, ob1, rb1))):
        all_of(0, got, which).wait_recv()
        out[...] = turn(got[...])
        send_hop(1, out, last, which)
    for g in range(2):
        begin(g)
        if g + 2 < EARLY:
            send_own(0, g + 2)

    all_of(1, rb0, 0).wait_recv()
    late_lines[0] = rb0[...].reshape(slots, early + 128)
    for copy in corrections:
        copy.start()
    arrived = rb0[:, :, early:].reshape(slots, 128)

    def node_of(numbers):
        numbers = numbers.astype(F32)
        return numbers[:, 0:1] * 16.0 + numbers[:, 64:65] - 1.0

    def selection(numbers):
        return one_hot(iota((rows, slots), 0) == to_row(node_of(numbers), slots).astype(jnp.int32))

    scatter[:, 2 * lines :] = selection(arrived)

    all_of(1, rb1, 1).wait_recv()
    for g in range(EARLY, GROUPS):
        set_near(hist_near[0, :, g * width : (g + 1) * width])
        rhs[2 * lines :] = rb1[:, :, (g - EARLY) * width : (g - EARLY + 1) * width].reshape(slots, width)
        inject(0, g, v[g], dot(scatter[...], rhs[...]))
        send_own(0, g)

    for g in range(2, EARLY):
        begin(g)
    for copy, on in zip(corrections, corrections_on):
        copy.wait_recv()
        on.start()
    all_of(0, ra2, 2).wait_recv()
    ob2[...] = turn(ra2[...])
    send_hop(1, ob2, rb2, 2)
    gather[lines:] = one_hot(iota((slots, rows), 1) == node_of(dot(swap[...], arrived)).astype(jnp.int32))

    def choose(place):
        chosen = dot(zr[:, place * rows : (place + 1) * rows], selection(late_lines[place, :, early:]))
        selected[:, place * slots : (place + 1) * slots] = chosen.astype(BF16)

    for place in range(3):
        choose(place)

    def finish(item):
        step, g = item // GROUPS, lax.rem(item, GROUPS)
        pair, side = g // 2, lax.rem(g, 2)
        at = pl.ds(pl.multiple_of(g * width, width), width)
        in_half = pl.ds(pl.multiple_of(side * width, width), width)
        v[g] = dot(zr[:, : 3 * rows], x[step, g, : 3 * rows])
        whole(step, g, 1, far_sem).wait_recv()
        v[g] += dot(zr[:, 3 * rows :], x[step, g, 3 * rows :])

        @pl.when((step == 0) & (g == 0))
        def _():
            for copy in corrections_on:
                copy.wait_recv()
            choose(3)

        @pl.when((step == 0) & (g < EARLY))
        def _():
            at = pl.ds(pl.multiple_of(lax.rem(g, EARLY) * width, width), width)
            v[g] += dot(selected[...], late_lines[:, :, at].reshape(4 * slots, width))

        @pl.when(step == 0)
        def _():
            @pl.when(g == 0)
            def _():
                all_of(1, rb2, 2).wait_recv()

            set_near(hist_near[1, :, at])
            rhs[2 * lines :] = rb2[:, :, at].reshape(slots, width)

        @pl.when((step == 1) | (step == 2))
        def _():
            which = (step - 1) * 2 + pair

            @pl.when(side == 0)
            def _():
                all_of(1, rb.at[which], 3 + which).wait_recv()

            rhs[2 * lines :] = rb[which, :, :block_b, in_half].reshape(slots, width)
            returned = rb[which, :, block_b:, in_half].reshape(slots, width)
            set_near(gain[...] * dot(slots_back[...], returned) - hist_far[step - 1, :, at])

        @pl.when(step < steps - 1)
        def _():
            inject(step + 1, g, v[g], dot(scatter[...], rhs[...]))
            send_own(step + 1, g)

        @pl.when(step == steps - 1)
        def _():
            pltpu.make_async_copy(v.at[g], out_hbm.at[:, at], out_sem.at[g]).start()

        @pl.when(step < 2)
        def _():
            which = step * 2 + pair
            volts = v[g]
            top = volts.astype(BF16)
            ends = dot(gather[...], top)
            near_volts = ends[:lines] + dot(gather[:lines], (volts - top.astype(F32)).astype(BF16))
            history = gain[...] * near_volts - hist_near[step, :, at]
            oa[which, :, :block_a, in_half] = (
                dot(slots_out[...], history.astype(BF16)).astype(BF16).reshape(zones, block_a, width)
            )
            oa[which, :, block_a:, in_half] = ends[lines:].astype(BF16).reshape(zones, block_a, width)

            @pl.when(side == 1)
            def _():
                send_hop(0, oa.at[which], ra.at[which], 3 + which)

        @pl.when((side == 0) & (item >= 2) & (item < 2 + 4 * 2))
        def _():
            which = item // 2 - 1
            all_of(0, ra.at[which], 3 + which).wait_recv()
            ob[which, :, :block_b] = turn(ra[which, :, :block_a])
            ob[which, :, block_b:] = turn(ra[which, :, block_a:])
            send_hop(1, ob.at[which], rb.at[which], 3 + which)

    def body(item, carry):
        @pl.when((item + AHEAD < items) & (item + AHEAD >= EARLY))
        def _():
            begin(item + AHEAD)

        finish(item)

        @pl.when(item >= GROUPS)
        def _():
            whole(item // GROUPS - 1, lax.rem(item, GROUPS), 3, far_sem).wait_send()

        return carry

    lax.fori_loop(0, items, body, 0)

    for g in range(GROUPS):
        whole(steps - 1, g, 3, far_sem).wait_send()
    for which, (sent_a, sent_b) in enumerate(((oa0, ob0), (oa1, ob1), (oa2, ob2))):
        all_of(0, sent_a, which).wait_send()
        all_of(1, sent_b, which).wait_send()
    for which in range(4):
        all_of(0, oa.at[which], 3 + which).wait_send()
        all_of(1, ob.at[which], 3 + which).wait_send()
    for copy in corrections + corrections_on:
        copy.wait_send()
    for g in range(GROUPS):
        at = pl.ds(g * width, width)
        pltpu.make_async_copy(v.at[g], out_hbm.at[:, at], out_sem.at[g]).wait()


def local(zones, subs, *arguments):
    (
        z_inverse,
        sources,
        v_start,
        hist_near,
        hist_far,
        switch_on,
        switch_cond,
        fault_node,
        fault_cond,
        remote_sub,
        near_node,
        far_node,
        line_gain,
    ) = arguments
    steps, _, rows, cases = sources.shape
    lines = near_node.shape[1]
    slots = 2 * zones * subs
    block_a, block_b = 2 * subs, 2 * zones
    width = cases // GROUPS
    half = 2 * width

    def exchange(wide, tall=1, count=None):
        lead = () if count is None else (count,)
        return [
            pltpu.VMEM(lead + (zones, tall * block_a, wide), BF16),
            pltpu.VMEM(lead + (zones, tall * block_a, wide), BF16),
            pltpu.VMEM(lead + (subs, tall * block_b, wide), BF16),
            pltpu.VMEM(lead + (subs, tall * block_b, wide), BF16),
        ]

    hbm = pl.BlockSpec(memory_space=pltpu.HBM)
    small = (
        switch_on,
        switch_cond,
        fault_node[None],
        fault_cond[None],
        remote_sub[:, :, 0],
        near_node,
        far_node,
        line_gain,
    )
    result = pl.pallas_call(
        functools.partial(kernel, zones, subs),
        out_shape=jax.ShapeDtypeStruct((rows, cases), F32),
        in_specs=[hbm] * (5 + len(small)),
        out_specs=hbm,
        scratch_shapes=[
            *(pltpu.VMEM(array.shape, array.dtype) for array in small),
            pltpu.VMEM((rows, 4 * rows), BF16),
            pltpu.VMEM((steps, GROUPS, 4 * rows, width), BF16),
            pltpu.VMEM((GROUPS, rows, width), F32),
            pltpu.VMEM((steps, rows, cases), BF16),
            pltpu.VMEM((2, lines, cases), F32),
            pltpu.VMEM((2, lines, cases), F32),
            pltpu.VMEM((steps, rows, width), F32),
            pltpu.VMEM((rows, 2 * lines + slots), BF16),
            pltpu.VMEM((lines + slots, rows), BF16),
            pltpu.VMEM((slots, lines), BF16),
            pltpu.VMEM((lines, slots), BF16),
            pltpu.VMEM((slots, slots), BF16),
            pltpu.VMEM((lines, width), F32),
            pltpu.VMEM((2 * lines + slots, width), BF16),
            *exchange(EARLY * width + 128),
            *exchange((GROUPS - EARLY) * width),
            *exchange(cases),
            *exchange(half, 2, 4),
            pltpu.VMEM((4, slots, EARLY * width + 128), BF16),
            pltpu.VMEM((rows, 4 * slots), BF16),
            pltpu.SemaphoreType.DMA((4,)),
            pltpu.SemaphoreType.DMA((4,)),
            pltpu.SemaphoreType.DMA((3 + GROUPS + 4 + 8,)),
            pltpu.SemaphoreType.DMA((steps, GROUPS)),
            pltpu.SemaphoreType.DMA((steps, GROUPS)),
            pltpu.SemaphoreType.DMA((steps, GROUPS)),
            pltpu.SemaphoreType.DMA((steps, GROUPS)),
            pltpu.SemaphoreType.DMA((7, 2)),
            pltpu.SemaphoreType.DMA((7, 2)),
            pltpu.SemaphoreType.DMA((GROUPS,)),
        ],
        compiler_params=pltpu.CompilerParams(
            collective_id=0, has_side_effects=True, vmem_limit_bytes=56 * 1024 * 1024
        ),
    )(
        z_inverse[0],
        sources[:, 0],
        v_start[0],
        hist_near[:, 0],
        hist_far[:, 0],
        *small,
    )
    return result[None]


def solution(mesh):
    placed = (
        P(("zone", "sub"), "row", None),
        P(None, ("zone", "sub"), "row", None),
        P(("zone", "sub"), "row", None),
        P(None, ("zone", "sub"), "row", None),
        P(None, ("zone", "sub"), "row", None),
        P(None, ("zone", "sub"), "row"),
        P(("zone", "sub"), "row"),
        P(),
        P(),
        P(("zone", "sub"), "row", None),
        P(("zone", "sub"), "row"),
        P(("zone", "sub"), "row"),
        P(("zone", "sub"), "row"),
    )
    return jax.shard_map(
        functools.partial(local, mesh.shape["zone"], mesh.shape["sub"]),
        mesh=mesh,
        in_specs=placed,
        out_specs=P(("zone", "sub"), "row", None),
        check_vma=False,
    )
```

```python
import functools

import jax
import jax.numpy as jnp
from jax import lax
from jax.experimental import pallas as pl
from jax.experimental.pallas import tpu as pltpu
from jax.sharding import PartitionSpec as P

MESH = pl.DeviceIdType.MESH
F32 = jnp.float32
BF16 = jnp.bfloat16
GROUPS = 4
EARLY = 2
AHEAD = 2


def dot(a, b):
    return jnp.dot(a, b, preferred_element_type=F32)


def iota(shape, dim):
    return lax.broadcasted_iota(jnp.int32, shape, dim)


def one_hot(mask):
    return jnp.where(mask, 1.0, 0.0).astype(BF16)


def to_column(row, size):
    eye = iota((size, size), 0) == iota((size, size), 1)
    return jnp.sum(jnp.where(eye, row, 0.0), axis=1, keepdims=True)


def to_row(column, size):
    eye = iota((size, size), 0) == iota((size, size), 1)
    return jnp.sum(jnp.where(eye, column, 0.0), axis=0, keepdims=True)


def kernel(
    zones,
    subs,
    z_hbm,
    src_hbm,
    vs_hbm,
    near_hbm,
    far_hbm,
    *rest,
):
    small_hbm, out_hbm, small, rest = rest[:8], rest[8], rest[9:17], rest[17:]
    (
        switch_on,
        switch_cond,
        fault_node,
        fault_cond,
        remote_sub,
        near_node,
        far_node,
        line_gain,
    ) = small
    (
        zr,
        x,
        v,
        src,
        hist_near,
        hist_far,
        switched,
        scatter,
        gather,
        slots_out,
        slots_back,
        swap,
        gain,
        rhs,
        oa0,
        ra0,
        ob0,
        rb0,
        oa1,
        ra1,
        ob1,
        rb1,
        oa2,
        ra2,
        ob2,
        rb2,
        oa,
        ra,
        ob,
        rb,
        late_lines,
        selected,
        fix_send,
        fix_recv,
        load_sem,
        send_sem,
        left_sem,
        right_sem,
        far_sem,
        ex_send,
        ex_recv,
        out_sem,
    ) = rest
    rows, nodes = z_hbm.shape
    steps, _, cases = src_hbm.shape
    lines = near_node.shape[1]
    slots = 2 * zones * subs
    block_a, block_b = 2 * subs, 2 * zones
    width = cases // GROUPS
    half = 2 * width
    early, late = EARLY * width, (GROUPS - EARLY) * width
    items = steps * GROUPS
    my_zone, my_sub, me = (lax.axis_index(name) for name in ("zone", "sub", "row"))
    right, left, across = lax.rem(me + 1, 4), lax.rem(me + 3, 4), lax.rem(me + 2, 4)

    barrier = pltpu.get_barrier_semaphore()
    for neighbour in (left, right):
        pl.semaphore_signal(barrier, inc=1, device_id={"row": neighbour}, device_id_type=MESH)
    for d in range(1, subs):
        pl.semaphore_signal(barrier, inc=1, device_id={"sub": lax.rem(my_sub + d, subs)}, device_id_type=MESH)
    for d in range(1, zones):
        pl.semaphore_signal(barrier, inc=1, device_id={"zone": lax.rem(my_zone + d, zones)}, device_id_type=MESH)

    order = (4, 6, 0, 1, 2, 3, 5, 7)
    loads = {
        number: pltpu.make_async_copy(small_hbm[number], small[number], load_sem.at[number]) for number in order
    }
    far_load = pltpu.make_async_copy(far_hbm, hist_far, load_sem.at[8])
    near_load = pltpu.make_async_copy(near_hbm, hist_near, load_sem.at[9])
    src_load = pltpu.make_async_copy(src_hbm, src, load_sem.at[10])
    start_loads = [
        pltpu.make_async_copy(vs_hbm.at[:, pl.ds(g * width, width)], v.at[g], load_sem.at[11 + g])
        for g in range(GROUPS)
    ]
    z_loads = []
    for place, origin in enumerate((me, left, right, across)):
        columns = pl.ds(pl.multiple_of(origin * rows, rows), rows)
        z_loads.append(
            pltpu.make_async_copy(
                z_hbm.at[:, columns], zr.at[:, pl.ds(place * rows, rows)], load_sem.at[11 + GROUPS + place]
            )
        )
    loads[4].start()
    loads[6].start()
    far_load.start()
    for number in order[2:]:
        loads[number].start()
    for load in [near_load, *start_loads, src_load, *z_loads]:
        load.start()

    loads[4].wait()
    loads[6].wait()

    target = remote_sub[...].astype(F32)
    target_col = to_column(target, lines)
    same = target_col == target
    first, second = iota((lines, lines), 0), iota((lines, lines), 1)
    rank = jnp.sum(jnp.where(same & (first < second), 1.0, 0.0), axis=0, keepdims=True)
    rank_col = jnp.sum(jnp.where(same & (second < first), 1.0, 0.0), axis=1, keepdims=True)
    target_int = remote_sub[...]
    slot_a = target_int * 2 + rank.astype(jnp.int32)
    zone_col = target_col.astype(jnp.int32) // subs
    sub_col = target_col.astype(jnp.int32) - zone_col * subs
    slot_b = sub_col * block_b + zone_col * 2 + rank_col.astype(jnp.int32)
    slots_out[...] = one_hot(iota((slots, lines), 0) == slot_a)
    slots_back[...] = one_hot(iota((lines, slots), 1) == slot_b)
    k = iota((slots, slots), 0)
    sub_of, rest = k // block_b, k - (k // block_b) * block_b
    swap[...] = one_hot(iota((slots, slots), 1) == (rest // 2) * block_a + sub_of * 2 + (rest - (rest // 2) * 2))
    far_col = (to_column(far_node[...].astype(F32), lines) + 1.0).astype(jnp.int32)
    high = far_col // 16
    numbers = jnp.where(iota((lines, 128), 1) < 64, high, far_col - high * 16).astype(F32).astype(BF16)
    numbers_out = dot(slots_out[...], numbers).astype(BF16)

    hops = (("zone", my_zone, zones), ("sub", my_sub, subs))

    def send_hop(phase, out, got, which):
        axis, my, size = hops[phase]
        got[pl.ds(my, 1)] = out[pl.ds(my, 1)]

        def one(d, carry):
            partner = lax.rem(my + d, size)
            pltpu.make_async_remote_copy(
                src_ref=out.at[partner],
                dst_ref=got.at[my],
                send_sem=ex_send.at[which, phase],
                recv_sem=ex_recv.at[which, phase],
                device_id={axis: partner},
                device_id_type=MESH,
            ).start()
            return carry

        lax.fori_loop(1, size, one, 0)

    def all_of(phase, buffer, which):
        axis, my, size = hops[phase]
        part = buffer.at[pl.ds(0, size - 1)]
        return pltpu.make_async_remote_copy(
            src_ref=part,
            dst_ref=part,
            send_sem=ex_send.at[which, phase],
            recv_sem=ex_recv.at[which, phase],
            device_id={axis: lax.rem(my + 1, size)},
            device_id_type=MESH,
        )

    def turn(got):
        values = got.reshape(slots, got.shape[-1])
        return dot(swap[...], values).astype(BF16).reshape(subs, block_b, got.shape[-1])

    far_load.wait()
    spread = slots_out[...]
    oa0[:, :, :early] = dot(spread, hist_far[0, :, :early].astype(BF16)).astype(BF16).reshape(zones, block_a, early)
    oa0[:, :, early:] = numbers_out.reshape(zones, block_a, 128)
    pl.semaphore_wait(barrier, 2 + subs - 1 + zones - 1)
    send_hop(0, oa0, ra0, 0)
    oa1[...] = dot(spread, hist_far[0, :, early:].astype(BF16)).astype(BF16).reshape(zones, block_a, late)
    send_hop(0, oa1, ra1, 1)

    for number in order[2:]:
        loads[number].wait()
    for load in [near_load, *start_loads, src_load]:
        load.wait()
    near_row = near_node[...]
    near_col = to_column(near_row.astype(F32), lines).astype(jnp.int32)
    near_matrix = one_hot(iota((rows, lines), 0) == near_row)
    scatter[:, :lines] = near_matrix
    scatter[:, lines : 2 * lines] = near_matrix
    gather[:lines] = one_hot(iota((lines, rows), 1) == near_col)
    gain[...] = jnp.broadcast_to(to_column(line_gain[...], lines), (lines, width))
    on = switch_on[:, 0].astype(F32) * switch_cond[...]
    eight = jnp.concatenate([on, jnp.zeros((8 - steps, rows), F32)], axis=0)
    columns = eight.T
    for step in range(steps):
        switched[step] = jnp.broadcast_to(columns[:, step : step + 1], (rows, width))

    def set_near(history):
        top = history.astype(BF16)
        rhs[:lines] = top
        rhs[lines : 2 * lines] = (history - top.astype(F32)).astype(BF16)

    def inject(step, g, volts, lines_in):
        at = pl.ds(pl.multiple_of(g * width, width), width)
        faulted = me * rows + iota((rows, width), 0) == fault_node[:, at]
        conduct = switched[step] + jnp.where(faulted, fault_cond[:, at], 0.0)
        x[step, g, :rows] = (src[step, :, at].astype(F32) + lines_in - conduct * volts).astype(BF16)

    def own_half(step, g, peer, place, sem, side):
        offset = side * (rows // 2)
        return pltpu.make_async_remote_copy(
            src_ref=x.at[step, g, pl.ds(offset, rows // 2)],
            dst_ref=x.at[step, g, pl.ds(place * rows + offset, rows // 2)],
            send_sem=send_sem.at[step, g],
            recv_sem=sem.at[step, g, side],
            device_id={"row": peer},
            device_id_type=MESH,
        )

    def send_own(step, g):
        for half_of in range(2):
            own_half(step, g, right, 1, left_sem, half_of).start()
            own_half(step, g, left, 2, right_sem, 1 - half_of).start()

    def pass_on(step, g, peer, place, offset):
        return pltpu.make_async_remote_copy(
            src_ref=x.at[step, g, pl.ds(place * rows + offset, rows // 2)],
            dst_ref=x.at[step, g, pl.ds(3 * rows + offset, rows // 2)],
            send_sem=send_sem.at[step, g],
            recv_sem=far_sem.at[step, g],
            device_id={"row": peer},
            device_id_type=MESH,
        )

    def whole(step, g, count, sem):
        part = x.at[step, g, pl.ds(0, count * rows)]
        return pltpu.make_async_remote_copy(
            src_ref=part,
            dst_ref=part,
            send_sem=send_sem.at[step, g],
            recv_sem=sem.at[step, g],
            device_id={"row": right},
            device_id_type=MESH,
        )

    def begin(item):
        step, g = item // GROUPS, lax.rem(item, GROUPS)
        own_half(step, g, right, 1, left_sem, 0).wait_recv()
        pass_on(step, g, right, 1, 0).start()
        own_half(step, g, left, 2, right_sem, 1).wait_recv()
        pass_on(step, g, left, 2, rows // 2).start()

    def correct(piece, peer, place):
        part = pl.ds(16 if piece else 0, slots if piece else 16 + slots)
        return pltpu.make_async_remote_copy(
            src_ref=late_lines.at[0, piece, part],
            dst_ref=late_lines.at[place, piece, part],
            send_sem=fix_send.at[piece, place - 1],
            recv_sem=fix_recv.at[piece, place - 1],
            device_id={"row": peer},
            device_id_type=MESH,
        )

    def correct_on(piece, peer, place):
        middle = 16 + slots // 2
        first = 16 if piece else 0
        part = pl.ds(first, middle - first) if place == 1 else pl.ds(middle, slots // 2)
        return pltpu.make_async_remote_copy(
            src_ref=late_lines.at[place, piece, part],
            dst_ref=late_lines.at[3, piece, part],
            send_sem=fix_send.at[piece, place + 1],
            recv_sem=fix_recv.at[piece, place + 1],
            device_id={"row": peer},
            device_id_type=MESH,
        )

    corrections = [(correct(piece, right, 1), correct(piece, left, 2)) for piece in range(EARLY)]
    corrections_on = [(correct_on(piece, right, 1), correct_on(piece, left, 2)) for piece in range(EARLY)]

    def correct_relay(piece):
        for copy, on in zip(corrections[piece], corrections_on[piece]):
            copy.wait_recv()
            on.start()

    def near_lines(g):
        set_near(hist_near[0, :, g * width : (g + 1) * width])

    for g in range(2):
        near_lines(g)
        inject(0, g, v[g], dot(scatter[:, : 2 * lines], rhs[: 2 * lines]))
        send_own(0, g)
    for which, (got, out, last) in enumerate(((ra0, ob0, rb0), (ra1, ob1, rb1))):
        all_of(0, got, which).wait_recv()
        out[...] = turn(got[...])
        send_hop(1, out, last, which)
    oa2[...] = dot(spread, hist_far[1].astype(BF16)).astype(BF16).reshape(zones, block_a, cases)
    send_hop(0, oa2, ra2, 2)
    for g in range(2, EARLY):
        near_lines(g)
        inject(0, g, v[g], dot(scatter[:, : 2 * lines], rhs[: 2 * lines]))
    for g in range(2):
        begin(g)
        if g + 2 < EARLY:
            send_own(0, g + 2)

    all_of(1, rb0, 0).wait_recv()
    arrived = rb0[:, :, early:].reshape(slots, 128)
    numbers = arrived.astype(F32)
    high_row, low_row = to_row(numbers[:, 0:1], slots), to_row(numbers[:, 64:65], slots)
    place_of = iota((16, slots), 0)
    node_rows = jnp.where(place_of == 0, high_row, jnp.where(place_of == 1, low_row, 0.0))
    late_lines[0, 0, :16, :slots] = node_rows.astype(BF16)
    for piece in range(EARLY):
        late_lines[0, piece, 16:] = rb0[:, :, piece * width : (piece + 1) * width].reshape(slots, width)
        for copy in corrections[piece]:
            copy.start()

    def selection(place):
        numbers = late_lines[place, 0, :16, :slots].astype(F32)
        node = (numbers[0:1] * 16.0 + numbers[1:2] - 1.0).astype(jnp.int32)
        return one_hot(iota((rows, slots), 0) == node)

    all_of(0, ra2, 2).wait_recv()
    ob2[...] = turn(ra2[...])
    send_hop(1, ob2, rb2, 2)
    scatter[:, 2 * lines :] = selection(0)

    all_of(1, rb1, 1).wait_recv()
    for g in range(EARLY, GROUPS):
        near_lines(g)
        rhs[2 * lines :] = rb1[:, :, (g - EARLY) * width : (g - EARLY + 1) * width].reshape(slots, width)
        inject(0, g, v[g], dot(scatter[...], rhs[...]))
    for g in range(GROUPS):
        if g < EARLY:
            correct_relay(g)
        if EARLY + g < GROUPS:
            send_own(0, EARLY + g)

    for g in range(2, EARLY):
        begin(g)
    turned = dot(swap[...], arrived)
    node_col = turned[:, 0:1] * 16.0 + turned[:, 64:65] - 1.0
    gather[lines:] = one_hot(iota((slots, rows), 1) == node_col.astype(jnp.int32))
    for load in z_loads:
        load.wait()

    def choose(place):
        chosen = dot(zr[:, place * rows : (place + 1) * rows], selection(place))
        selected[:, place * slots : (place + 1) * slots] = chosen.astype(BF16)

    for place in range(3):
        choose(place)

    def finish(item):
        step, g = item // GROUPS, lax.rem(item, GROUPS)
        pair, side = g // 2, lax.rem(g, 2)
        at = pl.ds(pl.multiple_of(g * width, width), width)
        in_half = pl.ds(pl.multiple_of(side * width, width), width)
        own_half(step, g, right, 1, left_sem, 1).wait_recv()
        own_half(step, g, left, 2, right_sem, 0).wait_recv()
        v[g] = dot(zr[:, : 3 * rows], x[step, g, : 3 * rows])
        whole(step, g, 1, far_sem).wait_recv()
        v[g] += dot(zr[:, 3 * rows :], x[step, g, 3 * rows :])

        @pl.when((step == 0) & (g == 0))
        def _():
            for copy in corrections_on[0]:
                copy.wait_recv()
            choose(3)

        for piece in range(EARLY):

            @pl.when((step == 0) & (g == piece))
            def _():
                if piece:
                    for copy in corrections_on[piece]:
                        copy.wait_recv()
                v[g] += dot(selected[...], late_lines[:, piece, 16:].reshape(4 * slots, width))

        @pl.when(step == 0)
        def _():
            @pl.when(g == 0)
            def _():
                all_of(1, rb2, 2).wait_recv()

            set_near(hist_near[1, :, at])
            rhs[2 * lines :] = rb2[:, :, at].reshape(slots, width)

        @pl.when((step == 1) | (step == 2))
        def _():
            which = (step - 1) * 2 + pair

            @pl.when(side == 0)
            def _():
                all_of(1, rb.at[which], 3 + which).wait_recv()

            rhs[2 * lines :] = rb[which, :, :block_b, in_half].reshape(slots, width)
            returned = rb[which, :, block_b:, in_half].reshape(slots, width)
            set_near(gain[...] * dot(slots_back[...], returned) - hist_far[step - 1, :, at])

        @pl.when(step < steps - 1)
        def _():
            inject(step + 1, g, v[g], dot(scatter[...], rhs[...]))
            send_own(step + 1, g)

        @pl.when(step == steps - 1)
        def _():
            pltpu.make_async_copy(v.at[g], out_hbm.at[:, at], out_sem.at[g]).start()

        @pl.when(step < 2)
        def _():
            which = step * 2 + pair
            volts = v[g]
            top = volts.astype(BF16)
            ends = dot(gather[...], top)
            near_volts = ends[:lines] + dot(gather[:lines], (volts - top.astype(F32)).astype(BF16))
            history = gain[...] * near_volts - hist_near[step, :, at]
            oa[which, :, :block_a, in_half] = (
                dot(slots_out[...], history.astype(BF16)).astype(BF16).reshape(zones, block_a, width)
            )
            oa[which, :, block_a:, in_half] = ends[lines:].astype(BF16).reshape(zones, block_a, width)

            @pl.when(side == 1)
            def _():
                send_hop(0, oa.at[which], ra.at[which], 3 + which)

        @pl.when((side == 0) & (item >= 2) & (item < 2 + 4 * 2))
        def _():
            which = item // 2 - 1
            all_of(0, ra.at[which], 3 + which).wait_recv()
            ob[which, :, :block_b] = turn(ra[which, :, :block_a])
            ob[which, :, block_b:] = turn(ra[which, :, block_a:])
            send_hop(1, ob.at[which], rb.at[which], 3 + which)

    def body(item, carry):
        @pl.when((item + AHEAD < items) & (item + AHEAD >= EARLY))
        def _():
            begin(item + AHEAD)

        finish(item)

        @pl.when(item >= GROUPS)
        def _():
            whole(item // GROUPS - 1, lax.rem(item, GROUPS), 3, far_sem).wait_send()

        return carry

    lax.fori_loop(0, items, body, 0)

    for g in range(GROUPS):
        whole(steps - 1, g, 3, far_sem).wait_send()
    for which, (sent_a, sent_b) in enumerate(((oa0, ob0), (oa1, ob1), (oa2, ob2))):
        all_of(0, sent_a, which).wait_send()
        all_of(1, sent_b, which).wait_send()
    for which in range(4):
        all_of(0, oa.at[which], 3 + which).wait_send()
        all_of(1, ob.at[which], 3 + which).wait_send()
    for pair in corrections + corrections_on:
        for copy in pair:
            copy.wait_send()
    for g in range(GROUPS):
        at = pl.ds(g * width, width)
        pltpu.make_async_copy(v.at[g], out_hbm.at[:, at], out_sem.at[g]).wait()


def local(zones, subs, *arguments):
    (
        z_inverse,
        sources,
        v_start,
        hist_near,
        hist_far,
        switch_on,
        switch_cond,
        fault_node,
        fault_cond,
        remote_sub,
        near_node,
        far_node,
        line_gain,
    ) = arguments
    steps, _, rows, cases = sources.shape
    lines = near_node.shape[1]
    slots = 2 * zones * subs
    block_a, block_b = 2 * subs, 2 * zones
    width = cases // GROUPS
    half = 2 * width

    def exchange(wide, tall=1, count=None):
        lead = () if count is None else (count,)
        return [
            pltpu.VMEM(lead + (zones, tall * block_a, wide), BF16),
            pltpu.VMEM(lead + (zones, tall * block_a, wide), BF16),
            pltpu.VMEM(lead + (subs, tall * block_b, wide), BF16),
            pltpu.VMEM(lead + (subs, tall * block_b, wide), BF16),
        ]

    hbm = pl.BlockSpec(memory_space=pltpu.HBM)
    small = (
        switch_on,
        switch_cond,
        fault_node[None],
        fault_cond[None],
        remote_sub[:, :, 0],
        near_node,
        far_node,
        line_gain,
    )
    result = pl.pallas_call(
        functools.partial(kernel, zones, subs),
        out_shape=jax.ShapeDtypeStruct((rows, cases), F32),
        in_specs=[hbm] * (5 + len(small)),
        out_specs=hbm,
        scratch_shapes=[
            *(pltpu.VMEM(array.shape, array.dtype) for array in small),
            pltpu.VMEM((rows, 4 * rows), BF16),
            pltpu.VMEM((steps, GROUPS, 4 * rows, width), BF16),
            pltpu.VMEM((GROUPS, rows, width), F32),
            pltpu.VMEM((steps, rows, cases), BF16),
            pltpu.VMEM((2, lines, cases), F32),
            pltpu.VMEM((2, lines, cases), F32),
            pltpu.VMEM((steps, rows, width), F32),
            pltpu.VMEM((rows, 2 * lines + slots), BF16),
            pltpu.VMEM((lines + slots, rows), BF16),
            pltpu.VMEM((slots, lines), BF16),
            pltpu.VMEM((lines, slots), BF16),
            pltpu.VMEM((slots, slots), BF16),
            pltpu.VMEM((lines, width), F32),
            pltpu.VMEM((2 * lines + slots, width), BF16),
            *exchange(EARLY * width + 128),
            *exchange((GROUPS - EARLY) * width),
            *exchange(cases),
            *exchange(half, 2, 4),
            pltpu.VMEM((4, EARLY, 16 + slots, width), BF16),
            pltpu.VMEM((rows, 4 * slots), BF16),
            pltpu.SemaphoreType.DMA((EARLY, 4)),
            pltpu.SemaphoreType.DMA((EARLY, 4)),
            pltpu.SemaphoreType.DMA((11 + GROUPS + 4,)),
            pltpu.SemaphoreType.DMA((steps, GROUPS)),
            pltpu.SemaphoreType.DMA((steps, GROUPS, 2)),
            pltpu.SemaphoreType.DMA((steps, GROUPS, 2)),
            pltpu.SemaphoreType.DMA((steps, GROUPS)),
            pltpu.SemaphoreType.DMA((7, 2)),
            pltpu.SemaphoreType.DMA((7, 2)),
            pltpu.SemaphoreType.DMA((GROUPS,)),
        ],
        compiler_params=pltpu.CompilerParams(
            collective_id=0, has_side_effects=True, vmem_limit_bytes=56 * 1024 * 1024
        ),
    )(
        z_inverse[0],
        sources[:, 0],
        v_start[0],
        hist_near[:, 0],
        hist_far[:, 0],
        *small,
    )
    return result[None]


def solution(mesh):
    placed = (
        P(("zone", "sub"), "row", None),
        P(None, ("zone", "sub"), "row", None),
        P(("zone", "sub"), "row", None),
        P(None, ("zone", "sub"), "row", None),
        P(None, ("zone", "sub"), "row", None),
        P(None, ("zone", "sub"), "row"),
        P(("zone", "sub"), "row"),
        P(),
        P(),
        P(("zone", "sub"), "row", None),
        P(("zone", "sub"), "row"),
        P(("zone", "sub"), "row"),
        P(("zone", "sub"), "row"),
    )
    return jax.shard_map(
        functools.partial(local, mesh.shape["zone"], mesh.shape["sub"]),
        mesh=mesh,
        in_specs=placed,
        out_specs=P(("zone", "sub"), "row", None),
        check_vma=False,
    )
```

```python
import functools

import jax
import jax.numpy as jnp
from jax import lax
from jax.experimental import pallas as pl
from jax.experimental.pallas import tpu as pltpu
from jax.sharding import PartitionSpec as P

MESH = pl.DeviceIdType.MESH
F32 = jnp.float32
BF16 = jnp.bfloat16
GROUPS = 4
EARLY = 2
AHEAD = 2


def dot(a, b):
    return jnp.dot(a, b, preferred_element_type=F32)


def iota(shape, dim):
    return lax.broadcasted_iota(jnp.int32, shape, dim)


def one_hot(mask):
    return jnp.where(mask, 1.0, 0.0).astype(BF16)


def to_column(row, size):
    eye = iota((size, size), 0) == iota((size, size), 1)
    return jnp.sum(jnp.where(eye, row, 0.0), axis=1, keepdims=True)


def to_row(column, size):
    eye = iota((size, size), 0) == iota((size, size), 1)
    return jnp.sum(jnp.where(eye, column, 0.0), axis=0, keepdims=True)


def kernel(
    zones,
    subs,
    z_hbm,
    src_hbm,
    vs_hbm,
    near_hbm,
    far_hbm,
    *rest,
):
    small_hbm, out_ref, small, rest = rest[:8], rest[8], rest[9:17], rest[17:]
    (
        switch_on,
        switch_cond,
        fault_node,
        fault_cond,
        remote_sub,
        near_node,
        far_node,
        line_gain,
    ) = small
    (
        zr,
        x,
        v,
        src,
        hist_near,
        hist_far,
        switched,
        scatter,
        gather,
        slots_out,
        slots_back,
        swap,
        gain,
        rhs,
        oa0,
        ra0,
        ob0,
        rb0,
        oa1,
        ra1,
        ob1,
        rb1,
        oa2,
        ra2,
        ob2,
        rb2,
        oa,
        ra,
        ob,
        rb,
        late_lines,
        selected,
        fix_send,
        fix_recv,
        load_sem,
        send_sem,
        left_sem,
        right_sem,
        far_sem,
        ex_send,
        ex_recv,
        out_sem,
    ) = rest
    rows, nodes = z_hbm.shape
    steps, _, cases = src_hbm.shape
    lines = near_node.shape[1]
    slots = 2 * zones * subs
    block_a, block_b = 2 * subs, 2 * zones
    width = cases // GROUPS
    early, late = EARLY * width, (GROUPS - EARLY) * width
    items = steps * GROUPS
    my_zone, my_sub, me = (lax.axis_index(name) for name in ("zone", "sub", "row"))
    right, left, across = lax.rem(me + 1, 4), lax.rem(me + 3, 4), lax.rem(me + 2, 4)

    barrier = pltpu.get_barrier_semaphore()
    for neighbour in (left, right):
        pl.semaphore_signal(barrier, inc=1, device_id={"row": neighbour}, device_id_type=MESH)
    for d in range(1, subs):
        pl.semaphore_signal(barrier, inc=1, device_id={"sub": lax.rem(my_sub + d, subs)}, device_id_type=MESH)
    for d in range(1, zones):
        pl.semaphore_signal(barrier, inc=1, device_id={"zone": lax.rem(my_zone + d, zones)}, device_id_type=MESH)

    order = (4, 6, 0, 1, 2, 3, 5, 7)
    loads = {
        number: pltpu.make_async_copy(small_hbm[number], small[number], load_sem.at[number]) for number in order
    }
    far_load = pltpu.make_async_copy(far_hbm, hist_far, load_sem.at[8])
    near_load = pltpu.make_async_copy(near_hbm, hist_near, load_sem.at[9])
    src_load = pltpu.make_async_copy(src_hbm, src, load_sem.at[10])
    start_loads = [
        pltpu.make_async_copy(vs_hbm.at[:, pl.ds(g * width, width)], v.at[g], load_sem.at[11 + g])
        for g in range(GROUPS)
    ]
    z_loads = []
    for place, origin in enumerate((me, left, right, across)):
        columns = pl.ds(pl.multiple_of(origin * rows, rows), rows)
        z_loads.append(
            pltpu.make_async_copy(
                z_hbm.at[:, columns], zr.at[:, pl.ds(place * rows, rows)], load_sem.at[11 + GROUPS + place]
            )
        )
    loads[4].start()
    loads[6].start()
    far_load.start()
    for number in order[2:]:
        loads[number].start()
    for load in [near_load, *start_loads, src_load, *z_loads]:
        load.start()

    loads[4].wait()
    loads[6].wait()

    target = remote_sub[...].astype(F32)
    target_col = to_column(target, lines)
    same = target_col == target
    first, second = iota((lines, lines), 0), iota((lines, lines), 1)
    rank = jnp.sum(jnp.where(same & (first < second), 1.0, 0.0), axis=0, keepdims=True)
    rank_col = jnp.sum(jnp.where(same & (second < first), 1.0, 0.0), axis=1, keepdims=True)
    target_int = remote_sub[...]
    slot_a = target_int * 2 + rank.astype(jnp.int32)
    zone_col = target_col.astype(jnp.int32) // subs
    sub_col = target_col.astype(jnp.int32) - zone_col * subs
    slot_b = sub_col * block_b + zone_col * 2 + rank_col.astype(jnp.int32)
    slots_out[...] = one_hot(iota((slots, lines), 0) == slot_a)
    slots_back[...] = one_hot(iota((lines, slots), 1) == slot_b)
    k = iota((slots, slots), 0)
    sub_of, rest = k // block_b, k - (k // block_b) * block_b
    swap[...] = one_hot(iota((slots, slots), 1) == (rest // 2) * block_a + sub_of * 2 + (rest - (rest // 2) * 2))
    far_col = (to_column(far_node[...].astype(F32), lines) + 1.0).astype(jnp.int32)
    high = far_col // 16
    numbers = jnp.where(iota((lines, 128), 1) < 64, high, far_col - high * 16).astype(F32).astype(BF16)
    numbers_out = dot(slots_out[...], numbers).astype(BF16)

    hops = (("zone", my_zone, zones), ("sub", my_sub, subs))

    def send_hop(phase, out, got, which):
        axis, my, size = hops[phase]
        got[pl.ds(my, 1)] = out[pl.ds(my, 1)]

        def one(d, carry):
            partner = lax.rem(my + d, size)
            pltpu.make_async_remote_copy(
                src_ref=out.at[partner],
                dst_ref=got.at[my],
                send_sem=ex_send.at[which, phase],
                recv_sem=ex_recv.at[which, phase],
                device_id={axis: partner},
                device_id_type=MESH,
            ).start()
            return carry

        lax.fori_loop(1, size, one, 0)

    def all_of(phase, buffer, which):
        axis, my, size = hops[phase]
        part = buffer.at[pl.ds(0, size - 1)]
        return pltpu.make_async_remote_copy(
            src_ref=part,
            dst_ref=part,
            send_sem=ex_send.at[which, phase],
            recv_sem=ex_recv.at[which, phase],
            device_id={axis: lax.rem(my + 1, size)},
            device_id_type=MESH,
        )

    def turn(got):
        values = got.reshape(slots, got.shape[-1])
        return dot(swap[...], values).astype(BF16).reshape(subs, block_b, got.shape[-1])

    far_load.wait()
    spread = slots_out[...]
    oa0[:, :, :early] = dot(spread, hist_far[0, :, :early].astype(BF16)).astype(BF16).reshape(zones, block_a, early)
    oa0[:, :, early:] = numbers_out.reshape(zones, block_a, 128)
    pl.semaphore_wait(barrier, 2 + subs - 1 + zones - 1)
    send_hop(0, oa0, ra0, 0)
    oa1[...] = dot(spread, hist_far[0, :, early:].astype(BF16)).astype(BF16).reshape(zones, block_a, late)
    send_hop(0, oa1, ra1, 1)

    for number in order[2:]:
        loads[number].wait()
    for load in [near_load, *start_loads, src_load]:
        load.wait()
    near_row = near_node[...]
    near_col = to_column(near_row.astype(F32), lines).astype(jnp.int32)
    near_matrix = one_hot(iota((rows, lines), 0) == near_row)
    scatter[:, :lines] = near_matrix
    scatter[:, lines : 2 * lines] = near_matrix
    gather[:lines] = one_hot(iota((lines, rows), 1) == near_col)
    gain[...] = jnp.broadcast_to(to_column(line_gain[...], lines), (lines, width))
    on = switch_on[:, 0].astype(F32) * switch_cond[...]
    eight = jnp.concatenate([on, jnp.zeros((8 - steps, rows), F32)], axis=0)
    columns = eight.T
    for step in range(steps):
        switched[step] = jnp.broadcast_to(columns[:, step : step + 1], (rows, width))

    def set_near(history):
        top = history.astype(BF16)
        rhs[:lines] = top
        rhs[lines : 2 * lines] = (history - top.astype(F32)).astype(BF16)

    def inject(step, g, volts, lines_in):
        at = pl.ds(pl.multiple_of(g * width, width), width)
        faulted = me * rows + iota((rows, width), 0) == fault_node[:, at]
        conduct = switched[step] + jnp.where(faulted, fault_cond[:, at], 0.0)
        x[step, g, :rows] = (src[step, :, at].astype(F32) + lines_in - conduct * volts).astype(BF16)

    def own_half(step, g, peer, place, sem, side):
        offset = side * (rows // 2)
        return pltpu.make_async_remote_copy(
            src_ref=x.at[step, g, pl.ds(offset, rows // 2)],
            dst_ref=x.at[step, g, pl.ds(place * rows + offset, rows // 2)],
            send_sem=send_sem.at[step, g],
            recv_sem=sem.at[step, g, side],
            device_id={"row": peer},
            device_id_type=MESH,
        )

    def send_own(step, g):
        for half_of in range(2):
            own_half(step, g, right, 1, left_sem, half_of).start()
            own_half(step, g, left, 2, right_sem, 1 - half_of).start()

    def pass_on(step, g, peer, place, offset):
        return pltpu.make_async_remote_copy(
            src_ref=x.at[step, g, pl.ds(place * rows + offset, rows // 2)],
            dst_ref=x.at[step, g, pl.ds(3 * rows + offset, rows // 2)],
            send_sem=send_sem.at[step, g],
            recv_sem=far_sem.at[step, g],
            device_id={"row": peer},
            device_id_type=MESH,
        )

    def whole(step, g, count, sem):
        part = x.at[step, g, pl.ds(0, count * rows)]
        return pltpu.make_async_remote_copy(
            src_ref=part,
            dst_ref=part,
            send_sem=send_sem.at[step, g],
            recv_sem=sem.at[step, g],
            device_id={"row": right},
            device_id_type=MESH,
        )

    def begin(item):
        step, g = item // GROUPS, lax.rem(item, GROUPS)
        own_half(step, g, right, 1, left_sem, 0).wait_recv()
        pass_on(step, g, right, 1, 0).start()
        own_half(step, g, left, 2, right_sem, 1).wait_recv()
        pass_on(step, g, left, 2, rows // 2).start()

    def correct(piece, peer, place):
        part = pl.ds(16 if piece else 0, slots if piece else 16 + slots)
        return pltpu.make_async_remote_copy(
            src_ref=late_lines.at[0, piece, part],
            dst_ref=late_lines.at[place, piece, part],
            send_sem=fix_send.at[piece, place - 1],
            recv_sem=fix_recv.at[piece, place - 1],
            device_id={"row": peer},
            device_id_type=MESH,
        )

    def correct_on(piece, peer, place):
        middle = 16 + slots // 2
        first = 16 if piece else 0
        part = pl.ds(first, middle - first) if place == 1 else pl.ds(middle, slots // 2)
        return pltpu.make_async_remote_copy(
            src_ref=late_lines.at[place, piece, part],
            dst_ref=late_lines.at[3, piece, part],
            send_sem=fix_send.at[piece, place + 1],
            recv_sem=fix_recv.at[piece, place + 1],
            device_id={"row": peer},
            device_id_type=MESH,
        )

    corrections = [(correct(piece, right, 1), correct(piece, left, 2)) for piece in range(EARLY)]
    corrections_on = [(correct_on(piece, right, 1), correct_on(piece, left, 2)) for piece in range(EARLY)]

    def correct_relay(piece):
        for copy, on in zip(corrections[piece], corrections_on[piece]):
            copy.wait_recv()
            on.start()

    def near_lines(g):
        set_near(hist_near[0, :, g * width : (g + 1) * width])

    for g in range(2):
        near_lines(g)
        inject(0, g, v[g], dot(scatter[:, : 2 * lines], rhs[: 2 * lines]))
        send_own(0, g)
    for which, (got, out, last) in enumerate(((ra0, ob0, rb0), (ra1, ob1, rb1))):
        all_of(0, got, which).wait_recv()
        out[...] = turn(got[...])
        send_hop(1, out, last, which)
    oa2[...] = dot(spread, hist_far[1].astype(BF16)).astype(BF16).reshape(zones, block_a, cases)
    send_hop(0, oa2, ra2, 2)
    for g in range(2, EARLY):
        near_lines(g)
        inject(0, g, v[g], dot(scatter[:, : 2 * lines], rhs[: 2 * lines]))
    for g in range(2):
        begin(g)
        if g + 2 < EARLY:
            send_own(0, g + 2)

    all_of(1, rb0, 0).wait_recv()
    arrived = rb0[:, :, early:].reshape(slots, 128)
    numbers = arrived.astype(F32)
    high_row, low_row = to_row(numbers[:, 0:1], slots), to_row(numbers[:, 64:65], slots)
    place_of = iota((16, slots), 0)
    node_rows = jnp.where(place_of == 0, high_row, jnp.where(place_of == 1, low_row, 0.0))
    late_lines[0, 0, :16, :slots] = node_rows.astype(BF16)
    for piece in range(EARLY):
        late_lines[0, piece, 16:] = rb0[:, :, piece * width : (piece + 1) * width].reshape(slots, width)
        for copy in corrections[piece]:
            copy.start()

    def selection(place):
        numbers = late_lines[place, 0, :16, :slots].astype(F32)
        node = (numbers[0:1] * 16.0 + numbers[1:2] - 1.0).astype(jnp.int32)
        return one_hot(iota((rows, slots), 0) == node)

    all_of(0, ra2, 2).wait_recv()
    ob2[...] = turn(ra2[...])
    send_hop(1, ob2, rb2, 2)
    scatter[:, 2 * lines :] = selection(0)

    all_of(1, rb1, 1).wait_recv()
    for g in range(EARLY, GROUPS):
        near_lines(g)
        rhs[2 * lines :] = rb1[:, :, (g - EARLY) * width : (g - EARLY + 1) * width].reshape(slots, width)
        inject(0, g, v[g], dot(scatter[...], rhs[...]))
    for g in range(GROUPS):
        if g < EARLY:
            correct_relay(g)
        if EARLY + g < GROUPS:
            send_own(0, EARLY + g)

    for g in range(2, EARLY):
        begin(g)
    turned = dot(swap[...], arrived)
    node_col = turned[:, 0:1] * 16.0 + turned[:, 64:65] - 1.0
    gather[lines:] = one_hot(iota((slots, rows), 1) == node_col.astype(jnp.int32))
    for load in z_loads:
        load.wait()

    def choose(place):
        chosen = dot(zr[:, place * rows : (place + 1) * rows], selection(place))
        selected[:, place * slots : (place + 1) * slots] = chosen.astype(BF16)

    for place in range(3):
        choose(place)

    def finish(item):
        step, g = item // GROUPS, lax.rem(item, GROUPS)
        at = pl.ds(pl.multiple_of(g * width, width), width)
        own_half(step, g, right, 1, left_sem, 1).wait_recv()
        own_half(step, g, left, 2, right_sem, 0).wait_recv()
        v[g] = dot(zr[:, : 3 * rows], x[step, g, : 3 * rows])
        whole(step, g, 1, far_sem).wait_recv()
        v[g] += dot(zr[:, 3 * rows :], x[step, g, 3 * rows :])

        @pl.when((step == 0) & (g == 0))
        def _():
            for copy in corrections_on[0]:
                copy.wait_recv()
            choose(3)

        for piece in range(EARLY):

            @pl.when((step == 0) & (g == piece))
            def _():
                if piece:
                    for copy in corrections_on[piece]:
                        copy.wait_recv()
                v[g] += dot(selected[...], late_lines[:, piece, 16:].reshape(4 * slots, width))

        @pl.when(step == 0)
        def _():
            @pl.when(g == 0)
            def _():
                all_of(1, rb2, 2).wait_recv()

            set_near(hist_near[1, :, at])
            rhs[2 * lines :] = rb2[:, :, at].reshape(slots, width)

        @pl.when((step == 1) | (step == 2))
        def _():
            which = item - GROUPS
            all_of(1, rb.at[which], 3 + which).wait_recv()
            rhs[2 * lines :] = rb[which, :, :block_b].reshape(slots, width)
            returned = rb[which, :, block_b:].reshape(slots, width)
            set_near(gain[...] * dot(slots_back[...], returned) - hist_far[step - 1, :, at])

        @pl.when(step < steps - 1)
        def _():
            inject(step + 1, g, v[g], dot(scatter[...], rhs[...]))
            send_own(step + 1, g)

        @pl.when(step == steps - 1)
        def _():
            pltpu.make_async_copy(v.at[g], out_ref.at[:, at], out_sem.at[g]).start()

        @pl.when(step < 2)
        def _():
            volts = v[g]
            top = volts.astype(BF16)
            ends = dot(gather[...], top)
            near_volts = ends[:lines] + dot(gather[:lines], (volts - top.astype(F32)).astype(BF16))
            history = gain[...] * near_volts - hist_near[step, :, at]
            oa[item, :, :block_a] = (
                dot(slots_out[...], history.astype(BF16)).astype(BF16).reshape(zones, block_a, width)
            )
            oa[item, :, block_a:] = ends[lines:].astype(BF16).reshape(zones, block_a, width)
            send_hop(0, oa.at[item], ra.at[item], 3 + item)

        @pl.when((item >= 1) & (item < 1 + 2 * GROUPS))
        def _():
            which = item - 1
            all_of(0, ra.at[which], 3 + which).wait_recv()
            ob[which, :, :block_b] = turn(ra[which, :, :block_a])
            ob[which, :, block_b:] = turn(ra[which, :, block_a:])
            send_hop(1, ob.at[which], rb.at[which], 3 + which)

    def body(item, carry):
        @pl.when((item + AHEAD < items) & (item + AHEAD >= EARLY))
        def _():
            begin(item + AHEAD)

        finish(item)

        @pl.when(item >= GROUPS)
        def _():
            whole(item // GROUPS - 1, lax.rem(item, GROUPS), 3, far_sem).wait_send()

        return carry

    lax.fori_loop(0, items, body, 0)

    for g in range(GROUPS):
        whole(steps - 1, g, 3, far_sem).wait_send()
    for which, (sent_a, sent_b) in enumerate(((oa0, ob0), (oa1, ob1), (oa2, ob2))):
        all_of(0, sent_a, which).wait_send()
        all_of(1, sent_b, which).wait_send()
    for which in range(2 * GROUPS):
        all_of(0, oa.at[which], 3 + which).wait_send()
        all_of(1, ob.at[which], 3 + which).wait_send()
    for pair in corrections + corrections_on:
        for copy in pair:
            copy.wait_send()
    for g in range(GROUPS):
        at = pl.ds(g * width, width)
        pltpu.make_async_copy(v.at[g], out_ref.at[:, at], out_sem.at[g]).wait()


def local(zones, subs, *arguments):
    (
        z_inverse,
        sources,
        v_start,
        hist_near,
        hist_far,
        switch_on,
        switch_cond,
        fault_node,
        fault_cond,
        remote_sub,
        near_node,
        far_node,
        line_gain,
    ) = arguments
    steps, _, rows, cases = sources.shape
    lines = near_node.shape[1]
    slots = 2 * zones * subs
    block_a, block_b = 2 * subs, 2 * zones
    width = cases // GROUPS

    def exchange(wide, tall=1, count=None):
        lead = () if count is None else (count,)
        return [
            pltpu.VMEM(lead + (zones, tall * block_a, wide), BF16),
            pltpu.VMEM(lead + (zones, tall * block_a, wide), BF16),
            pltpu.VMEM(lead + (subs, tall * block_b, wide), BF16),
            pltpu.VMEM(lead + (subs, tall * block_b, wide), BF16),
        ]

    hbm = pl.BlockSpec(memory_space=pltpu.HBM)
    small = (
        switch_on,
        switch_cond,
        fault_node[None],
        fault_cond[None],
        remote_sub[:, :, 0],
        near_node,
        far_node,
        line_gain,
    )
    result = pl.pallas_call(
        functools.partial(kernel, zones, subs),
        out_shape=pltpu.VMEM((rows, cases), F32),
        in_specs=[hbm] * (5 + len(small)),
        out_specs=pl.BlockSpec(memory_space=pl.ANY),
        scratch_shapes=[
            *(pltpu.VMEM(array.shape, array.dtype) for array in small),
            pltpu.VMEM((rows, 4 * rows), BF16),
            pltpu.VMEM((steps, GROUPS, 4 * rows, width), BF16),
            pltpu.VMEM((GROUPS, rows, width), F32),
            pltpu.VMEM((steps, rows, cases), BF16),
            pltpu.VMEM((2, lines, cases), F32),
            pltpu.VMEM((2, lines, cases), F32),
            pltpu.VMEM((steps, rows, width), F32),
            pltpu.VMEM((rows, 2 * lines + slots), BF16),
            pltpu.VMEM((lines + slots, rows), BF16),
            pltpu.VMEM((slots, lines), BF16),
            pltpu.VMEM((lines, slots), BF16),
            pltpu.VMEM((slots, slots), BF16),
            pltpu.VMEM((lines, width), F32),
            pltpu.VMEM((2 * lines + slots, width), BF16),
            *exchange(EARLY * width + 128),
            *exchange((GROUPS - EARLY) * width),
            *exchange(cases),
            *exchange(width, 2, 2 * GROUPS),
            pltpu.VMEM((4, EARLY, 16 + slots, width), BF16),
            pltpu.VMEM((rows, 4 * slots), BF16),
            pltpu.SemaphoreType.DMA((EARLY, 4)),
            pltpu.SemaphoreType.DMA((EARLY, 4)),
            pltpu.SemaphoreType.DMA((11 + GROUPS + 4,)),
            pltpu.SemaphoreType.DMA((steps, GROUPS)),
            pltpu.SemaphoreType.DMA((steps, GROUPS, 2)),
            pltpu.SemaphoreType.DMA((steps, GROUPS, 2)),
            pltpu.SemaphoreType.DMA((steps, GROUPS)),
            pltpu.SemaphoreType.DMA((3 + 2 * GROUPS, 2)),
            pltpu.SemaphoreType.DMA((3 + 2 * GROUPS, 2)),
            pltpu.SemaphoreType.DMA((GROUPS,)),
        ],
        compiler_params=pltpu.CompilerParams(
            collective_id=0, has_side_effects=True, vmem_limit_bytes=56 * 1024 * 1024
        ),
    )(
        z_inverse[0],
        sources[:, 0],
        v_start[0],
        hist_near[:, 0],
        hist_far[:, 0],
        *small,
    )
    return result[None]


def solution(mesh):
    placed = (
        P(("zone", "sub"), "row", None),
        P(None, ("zone", "sub"), "row", None),
        P(("zone", "sub"), "row", None),
        P(None, ("zone", "sub"), "row", None),
        P(None, ("zone", "sub"), "row", None),
        P(None, ("zone", "sub"), "row"),
        P(("zone", "sub"), "row"),
        P(),
        P(),
        P(("zone", "sub"), "row", None),
        P(("zone", "sub"), "row"),
        P(("zone", "sub"), "row"),
        P(("zone", "sub"), "row"),
    )
    return jax.shard_map(
        functools.partial(local, mesh.shape["zone"], mesh.shape["sub"]),
        mesh=mesh,
        in_specs=placed,
        out_specs=P(("zone", "sub"), "row", None),
        check_vma=False,
    )
```

```python
import functools

import jax
import jax.numpy as jnp
from jax import lax
from jax.experimental import pallas as pl
from jax.experimental.pallas import tpu as pltpu
from jax.sharding import PartitionSpec as P

MESH = pl.DeviceIdType.MESH
F32 = jnp.float32
BF16 = jnp.bfloat16
GROUPS = 4
EARLY = 2
AHEAD = 2


def dot(a, b):
    return jnp.dot(a, b, preferred_element_type=F32)


def iota(shape, dim):
    return lax.broadcasted_iota(jnp.int32, shape, dim)


def one_hot(mask):
    return jnp.where(mask, 1.0, 0.0).astype(BF16)


def to_column(row, size):
    eye = iota((size, size), 0) == iota((size, size), 1)
    return jnp.sum(jnp.where(eye, row, 0.0), axis=1, keepdims=True)


def to_row(column, size):
    eye = iota((size, size), 0) == iota((size, size), 1)
    return jnp.sum(jnp.where(eye, column, 0.0), axis=0, keepdims=True)


def kernel(
    zones,
    subs,
    z_hbm,
    src_hbm,
    vs_hbm,
    near_hbm,
    far_hbm,
    *rest,
):
    small_hbm, out_ref, small, rest = rest[:8], rest[8], rest[9:17], rest[17:]
    (
        switch_on,
        switch_cond,
        fault_node,
        fault_cond,
        remote_sub,
        near_node,
        far_node,
        line_gain,
    ) = small
    (
        zr,
        x,
        v,
        src,
        hist_near,
        hist_far,
        switched,
        scatter,
        gather,
        slots_out,
        slots_back,
        swap,
        gain,
        rhs,
        oa0,
        ra0,
        ob0,
        rb0,
        oa1,
        ra1,
        ob1,
        rb1,
        oa2,
        ra2,
        ob2,
        rb2,
        oa,
        ra,
        ob,
        rb,
        late_lines,
        selected,
        fix_send,
        fix_recv,
        load_sem,
        send_sem,
        left_sem,
        right_sem,
        far_sem,
        ex_send,
        ex_recv,
    ) = rest
    rows, nodes = z_hbm.shape
    steps, _, cases = src_hbm.shape
    lines = near_node.shape[1]
    slots = 2 * zones * subs
    block_a, block_b = 2 * subs, 2 * zones
    width = cases // GROUPS
    early, late = EARLY * width, (GROUPS - EARLY) * width
    items = steps * GROUPS
    my_zone, my_sub, me = (lax.axis_index(name) for name in ("zone", "sub", "row"))
    right, left, across = lax.rem(me + 1, 4), lax.rem(me + 3, 4), lax.rem(me + 2, 4)

    barrier = pltpu.get_barrier_semaphore()
    for neighbour in (left, right):
        pl.semaphore_signal(barrier, inc=1, device_id={"row": neighbour}, device_id_type=MESH)
    for d in range(1, subs):
        pl.semaphore_signal(barrier, inc=1, device_id={"sub": lax.rem(my_sub + d, subs)}, device_id_type=MESH)
    for d in range(1, zones):
        pl.semaphore_signal(barrier, inc=1, device_id={"zone": lax.rem(my_zone + d, zones)}, device_id_type=MESH)

    order = (4, 6, 0, 1, 2, 3, 5, 7)
    loads = {
        number: pltpu.make_async_copy(small_hbm[number], small[number], load_sem.at[number]) for number in order
    }
    far_load = pltpu.make_async_copy(far_hbm, hist_far, load_sem.at[8])
    near_load = pltpu.make_async_copy(near_hbm, hist_near, load_sem.at[9])
    src_load = pltpu.make_async_copy(src_hbm, src, load_sem.at[10])
    start_loads = [
        pltpu.make_async_copy(vs_hbm.at[:, pl.ds(g * width, width)], v.at[g], load_sem.at[11 + g])
        for g in range(GROUPS)
    ]
    z_loads = []
    for place, origin in enumerate((me, left, right, across)):
        columns = pl.ds(pl.multiple_of(origin * rows, rows), rows)
        z_loads.append(
            pltpu.make_async_copy(
                z_hbm.at[:, columns], zr.at[:, pl.ds(place * rows, rows)], load_sem.at[11 + GROUPS + place]
            )
        )
    loads[4].start()
    loads[6].start()
    far_load.start()
    for number in order[2:]:
        loads[number].start()
    for load in [near_load, *start_loads, src_load, *z_loads]:
        load.start()

    loads[4].wait()
    loads[6].wait()

    target = remote_sub[...].astype(F32)
    target_col = to_column(target, lines)
    same = target_col == target
    first, second = iota((lines, lines), 0), iota((lines, lines), 1)
    rank = jnp.sum(jnp.where(same & (first < second), 1.0, 0.0), axis=0, keepdims=True)
    rank_col = jnp.sum(jnp.where(same & (second < first), 1.0, 0.0), axis=1, keepdims=True)
    target_int = remote_sub[...]
    slot_a = target_int * 2 + rank.astype(jnp.int32)
    zone_col = target_col.astype(jnp.int32) // subs
    sub_col = target_col.astype(jnp.int32) - zone_col * subs
    slot_b = sub_col * block_b + zone_col * 2 + rank_col.astype(jnp.int32)
    slots_out[...] = one_hot(iota((slots, lines), 0) == slot_a)
    slots_back[...] = one_hot(iota((lines, slots), 1) == slot_b)
    k = iota((slots, slots), 0)
    sub_of, rest = k // block_b, k - (k // block_b) * block_b
    swap[...] = one_hot(iota((slots, slots), 1) == (rest // 2) * block_a + sub_of * 2 + (rest - (rest // 2) * 2))
    far_col = (to_column(far_node[...].astype(F32), lines) + 1.0).astype(jnp.int32)
    high = far_col // 16
    numbers = jnp.where(iota((lines, 128), 1) < 64, high, far_col - high * 16).astype(F32).astype(BF16)
    numbers_out = dot(slots_out[...], numbers).astype(BF16)

    hops = (("zone", my_zone, zones), ("sub", my_sub, subs))

    def send_hop(phase, out, got, which):
        axis, my, size = hops[phase]
        got[pl.ds(my, 1)] = out[pl.ds(my, 1)]

        def one(d, carry):
            partner = lax.rem(my + d, size)
            pltpu.make_async_remote_copy(
                src_ref=out.at[partner],
                dst_ref=got.at[my],
                send_sem=ex_send.at[which, phase],
                recv_sem=ex_recv.at[which, phase],
                device_id={axis: partner},
                device_id_type=MESH,
            ).start()
            return carry

        lax.fori_loop(1, size, one, 0)

    def all_of(phase, buffer, which):
        axis, my, size = hops[phase]
        part = buffer.at[pl.ds(0, size - 1)]
        return pltpu.make_async_remote_copy(
            src_ref=part,
            dst_ref=part,
            send_sem=ex_send.at[which, phase],
            recv_sem=ex_recv.at[which, phase],
            device_id={axis: lax.rem(my + 1, size)},
            device_id_type=MESH,
        )

    def turn(got):
        values = got.reshape(slots, got.shape[-1])
        return dot(swap[...], values).astype(BF16).reshape(subs, block_b, got.shape[-1])

    far_load.wait()
    spread = slots_out[...]
    oa0[:, :, :early] = dot(spread, hist_far[0, :, :early].astype(BF16)).astype(BF16).reshape(zones, block_a, early)
    oa0[:, :, early:] = numbers_out.reshape(zones, block_a, 128)
    pl.semaphore_wait(barrier, 2 + subs - 1 + zones - 1)
    send_hop(0, oa0, ra0, 0)
    oa1[...] = dot(spread, hist_far[0, :, early:].astype(BF16)).astype(BF16).reshape(zones, block_a, late)
    send_hop(0, oa1, ra1, 1)

    for number in order[2:]:
        loads[number].wait()
    for load in [near_load, *start_loads, src_load]:
        load.wait()
    near_row = near_node[...]
    near_col = to_column(near_row.astype(F32), lines).astype(jnp.int32)
    near_matrix = one_hot(iota((rows, lines), 0) == near_row)
    scatter[:, :lines] = near_matrix
    scatter[:, lines : 2 * lines] = near_matrix
    gather[:lines] = one_hot(iota((lines, rows), 1) == near_col)
    gain[...] = jnp.broadcast_to(to_column(line_gain[...], lines), (lines, width))
    on = switch_on[:, 0].astype(F32) * switch_cond[...]
    eight = jnp.concatenate([on, jnp.zeros((8 - steps, rows), F32)], axis=0)
    columns = eight.T
    for step in range(steps):
        switched[step] = jnp.broadcast_to(columns[:, step : step + 1], (rows, width))

    def set_near(history):
        top = history.astype(BF16)
        rhs[:lines] = top
        rhs[lines : 2 * lines] = (history - top.astype(F32)).astype(BF16)

    def inject(step, g, volts, lines_in):
        at = pl.ds(pl.multiple_of(g * width, width), width)
        faulted = me * rows + iota((rows, width), 0) == fault_node[:, at]
        conduct = switched[step] + jnp.where(faulted, fault_cond[:, at], 0.0)
        x[step, g, :rows] = (src[step, :, at].astype(F32) + lines_in - conduct * volts).astype(BF16)

    def own_half(step, g, peer, place, sem, side):
        offset = side * (rows // 2)
        return pltpu.make_async_remote_copy(
            src_ref=x.at[step, g, pl.ds(offset, rows // 2)],
            dst_ref=x.at[step, g, pl.ds(place * rows + offset, rows // 2)],
            send_sem=send_sem.at[step, g],
            recv_sem=sem.at[step, g, side],
            device_id={"row": peer},
            device_id_type=MESH,
        )

    def send_own(step, g):
        for half_of in range(2):
            own_half(step, g, right, 1, left_sem, half_of).start()
            own_half(step, g, left, 2, right_sem, 1 - half_of).start()

    def pass_on(step, g, peer, place, offset):
        return pltpu.make_async_remote_copy(
            src_ref=x.at[step, g, pl.ds(place * rows + offset, rows // 2)],
            dst_ref=x.at[step, g, pl.ds(3 * rows + offset, rows // 2)],
            send_sem=send_sem.at[step, g],
            recv_sem=far_sem.at[step, g],
            device_id={"row": peer},
            device_id_type=MESH,
        )

    def whole(step, g, count, sem):
        part = x.at[step, g, pl.ds(0, count * rows)]
        return pltpu.make_async_remote_copy(
            src_ref=part,
            dst_ref=part,
            send_sem=send_sem.at[step, g],
            recv_sem=sem.at[step, g],
            device_id={"row": right},
            device_id_type=MESH,
        )

    def begin(item):
        step, g = item // GROUPS, lax.rem(item, GROUPS)
        own_half(step, g, right, 1, left_sem, 0).wait_recv()
        pass_on(step, g, right, 1, 0).start()
        own_half(step, g, left, 2, right_sem, 1).wait_recv()
        pass_on(step, g, left, 2, rows // 2).start()

    def correct(piece, peer, place):
        part = pl.ds(16 if piece else 0, slots if piece else 16 + slots)
        return pltpu.make_async_remote_copy(
            src_ref=late_lines.at[0, piece, part],
            dst_ref=late_lines.at[place, piece, part],
            send_sem=fix_send.at[piece, place - 1],
            recv_sem=fix_recv.at[piece, place - 1],
            device_id={"row": peer},
            device_id_type=MESH,
        )

    def correct_on(piece, peer, place):
        middle = 16 + slots // 2
        first = 16 if piece else 0
        part = pl.ds(first, middle - first) if place == 1 else pl.ds(middle, slots // 2)
        return pltpu.make_async_remote_copy(
            src_ref=late_lines.at[place, piece, part],
            dst_ref=late_lines.at[3, piece, part],
            send_sem=fix_send.at[piece, place + 1],
            recv_sem=fix_recv.at[piece, place + 1],
            device_id={"row": peer},
            device_id_type=MESH,
        )

    corrections = [(correct(piece, right, 1), correct(piece, left, 2)) for piece in range(EARLY)]
    corrections_on = [(correct_on(piece, right, 1), correct_on(piece, left, 2)) for piece in range(EARLY)]

    def correct_relay(piece):
        for copy, on in zip(corrections[piece], corrections_on[piece]):
            copy.wait_recv()
            on.start()

    def near_lines(g):
        set_near(hist_near[0, :, g * width : (g + 1) * width])

    for g in range(2):
        near_lines(g)
        inject(0, g, v[g], dot(scatter[:, : 2 * lines], rhs[: 2 * lines]))
        send_own(0, g)
    for which, (got, out, last) in enumerate(((ra0, ob0, rb0), (ra1, ob1, rb1))):
        all_of(0, got, which).wait_recv()
        out[...] = turn(got[...])
        send_hop(1, out, last, which)
    oa2[...] = dot(spread, hist_far[1].astype(BF16)).astype(BF16).reshape(zones, block_a, cases)
    send_hop(0, oa2, ra2, 2)
    for g in range(2, EARLY):
        near_lines(g)
        inject(0, g, v[g], dot(scatter[:, : 2 * lines], rhs[: 2 * lines]))
    for g in range(2):
        begin(g)
        if g + 2 < EARLY:
            send_own(0, g + 2)

    all_of(1, rb0, 0).wait_recv()
    arrived = rb0[:, :, early:].reshape(slots, 128)
    numbers = arrived.astype(F32)
    high_row, low_row = to_row(numbers[:, 0:1], slots), to_row(numbers[:, 64:65], slots)
    place_of = iota((16, slots), 0)
    node_rows = jnp.where(place_of == 0, high_row, jnp.where(place_of == 1, low_row, 0.0))
    late_lines[0, 0, :16, :slots] = node_rows.astype(BF16)
    for piece in range(EARLY):
        late_lines[0, piece, 16:] = rb0[:, :, piece * width : (piece + 1) * width].reshape(slots, width)
        for copy in corrections[piece]:
            copy.start()

    def selection(place):
        numbers = late_lines[place, 0, :16, :slots].astype(F32)
        node = (numbers[0:1] * 16.0 + numbers[1:2] - 1.0).astype(jnp.int32)
        return one_hot(iota((rows, slots), 0) == node)

    all_of(0, ra2, 2).wait_recv()
    ob2[...] = turn(ra2[...])
    send_hop(1, ob2, rb2, 2)
    scatter[:, 2 * lines :] = selection(0)

    all_of(1, rb1, 1).wait_recv()
    for g in range(EARLY, GROUPS):
        near_lines(g)
        rhs[2 * lines :] = rb1[:, :, (g - EARLY) * width : (g - EARLY + 1) * width].reshape(slots, width)
        inject(0, g, v[g], dot(scatter[...], rhs[...]))
    for g in range(GROUPS):
        if g < EARLY:
            correct_relay(g)
        if EARLY + g < GROUPS:
            send_own(0, EARLY + g)

    for g in range(2, EARLY):
        begin(g)
    turned = dot(swap[...], arrived)
    node_col = turned[:, 0:1] * 16.0 + turned[:, 64:65] - 1.0
    gather[lines:] = one_hot(iota((slots, rows), 1) == node_col.astype(jnp.int32))
    for load in z_loads:
        load.wait()

    def choose(place):
        chosen = dot(zr[:, place * rows : (place + 1) * rows], selection(place))
        selected[:, place * slots : (place + 1) * slots] = chosen.astype(BF16)

    for place in range(3):
        choose(place)

    def finish(item):
        step, g = item // GROUPS, lax.rem(item, GROUPS)
        at = pl.ds(pl.multiple_of(g * width, width), width)
        own_half(step, g, right, 1, left_sem, 1).wait_recv()
        own_half(step, g, left, 2, right_sem, 0).wait_recv()
        v[g] = dot(zr[:, : 3 * rows], x[step, g, : 3 * rows])
        whole(step, g, 1, far_sem).wait_recv()
        v[g] += dot(zr[:, 3 * rows :], x[step, g, 3 * rows :])

        @pl.when((step == 0) & (g == 0))
        def _():
            for copy in corrections_on[0]:
                copy.wait_recv()
            choose(3)

        for piece in range(EARLY):

            @pl.when((step == 0) & (g == piece))
            def _():
                if piece:
                    for copy in corrections_on[piece]:
                        copy.wait_recv()
                v[g] += dot(selected[...], late_lines[:, piece, 16:].reshape(4 * slots, width))

        @pl.when(step == 0)
        def _():
            @pl.when(g == 0)
            def _():
                all_of(1, rb2, 2).wait_recv()

            set_near(hist_near[1, :, at])
            rhs[2 * lines :] = rb2[:, :, at].reshape(slots, width)

        @pl.when((step == 1) | (step == 2))
        def _():
            which = item - GROUPS
            all_of(1, rb.at[which], 3 + which).wait_recv()
            rhs[2 * lines :] = rb[which, :, :block_b].reshape(slots, width)
            returned = rb[which, :, block_b:].reshape(slots, width)
            set_near(gain[...] * dot(slots_back[...], returned) - hist_far[step - 1, :, at])

        @pl.when(step < steps - 1)
        def _():
            inject(step + 1, g, v[g], dot(scatter[...], rhs[...]))
            send_own(step + 1, g)

        @pl.when(step == steps - 1)
        def _():
            out_ref[:, at] = v[g]

        @pl.when(step < 2)
        def _():
            volts = v[g]
            top = volts.astype(BF16)
            ends = dot(gather[...], top)
            near_volts = ends[:lines] + dot(gather[:lines], (volts - top.astype(F32)).astype(BF16))
            history = gain[...] * near_volts - hist_near[step, :, at]
            oa[item, :, :block_a] = (
                dot(slots_out[...], history.astype(BF16)).astype(BF16).reshape(zones, block_a, width)
            )
            oa[item, :, block_a:] = ends[lines:].astype(BF16).reshape(zones, block_a, width)
            send_hop(0, oa.at[item], ra.at[item], 3 + item)

        @pl.when((item >= 1) & (item < 1 + 2 * GROUPS))
        def _():
            which = item - 1
            all_of(0, ra.at[which], 3 + which).wait_recv()
            ob[which, :, :block_b] = turn(ra[which, :, :block_a])
            ob[which, :, block_b:] = turn(ra[which, :, block_a:])
            send_hop(1, ob.at[which], rb.at[which], 3 + which)

    def body(item, carry):
        @pl.when(item == items - 3)
        def _():
            for which, (sent_a, sent_b) in enumerate(((oa0, ob0), (oa1, ob1), (oa2, ob2))):
                all_of(0, sent_a, which).wait_send()
                all_of(1, sent_b, which).wait_send()
            for which in range(2 * GROUPS):
                all_of(0, oa.at[which], 3 + which).wait_send()
                all_of(1, ob.at[which], 3 + which).wait_send()
            for pair in corrections + corrections_on:
                for copy in pair:
                    copy.wait_send()

        @pl.when((item + AHEAD < items) & (item + AHEAD >= EARLY))
        def _():
            begin(item + AHEAD)

        finish(item)

        @pl.when(item >= GROUPS)
        def _():
            whole(item // GROUPS - 1, lax.rem(item, GROUPS), 3, far_sem).wait_send()

        return carry

    lax.fori_loop(0, items, body, 0)

    for g in range(GROUPS):
        whole(steps - 1, g, 3, far_sem).wait_send()


def local(zones, subs, *arguments):
    (
        z_inverse,
        sources,
        v_start,
        hist_near,
        hist_far,
        switch_on,
        switch_cond,
        fault_node,
        fault_cond,
        remote_sub,
        near_node,
        far_node,
        line_gain,
    ) = arguments
    steps, _, rows, cases = sources.shape
    lines = near_node.shape[1]
    slots = 2 * zones * subs
    block_a, block_b = 2 * subs, 2 * zones
    width = cases // GROUPS

    def exchange(wide, tall=1, count=None):
        lead = () if count is None else (count,)
        return [
            pltpu.VMEM(lead + (zones, tall * block_a, wide), BF16),
            pltpu.VMEM(lead + (zones, tall * block_a, wide), BF16),
            pltpu.VMEM(lead + (subs, tall * block_b, wide), BF16),
            pltpu.VMEM(lead + (subs, tall * block_b, wide), BF16),
        ]

    hbm = pl.BlockSpec(memory_space=pltpu.HBM)
    small = (
        switch_on,
        switch_cond,
        fault_node[None],
        fault_cond[None],
        remote_sub[:, :, 0],
        near_node,
        far_node,
        line_gain,
    )
    result = pl.pallas_call(
        functools.partial(kernel, zones, subs),
        out_shape=pltpu.VMEM((rows, cases), F32),
        in_specs=[hbm] * (5 + len(small)),
        out_specs=pl.BlockSpec(memory_space=pltpu.VMEM),
        scratch_shapes=[
            *(pltpu.VMEM(array.shape, array.dtype) for array in small),
            pltpu.VMEM((rows, 4 * rows), BF16),
            pltpu.VMEM((steps, GROUPS, 4 * rows, width), BF16),
            pltpu.VMEM((GROUPS, rows, width), F32),
            pltpu.VMEM((steps, rows, cases), BF16),
            pltpu.VMEM((2, lines, cases), F32),
            pltpu.VMEM((2, lines, cases), F32),
            pltpu.VMEM((steps, rows, width), F32),
            pltpu.VMEM((rows, 2 * lines + slots), BF16),
            pltpu.VMEM((lines + slots, rows), BF16),
            pltpu.VMEM((slots, lines), BF16),
            pltpu.VMEM((lines, slots), BF16),
            pltpu.VMEM((slots, slots), BF16),
            pltpu.VMEM((lines, width), F32),
            pltpu.VMEM((2 * lines + slots, width), BF16),
            *exchange(EARLY * width + 128),
            *exchange((GROUPS - EARLY) * width),
            *exchange(cases),
            *exchange(width, 2, 2 * GROUPS),
            pltpu.VMEM((4, EARLY, 16 + slots, width), BF16),
            pltpu.VMEM((rows, 4 * slots), BF16),
            pltpu.SemaphoreType.DMA((EARLY, 4)),
            pltpu.SemaphoreType.DMA((EARLY, 4)),
            pltpu.SemaphoreType.DMA((11 + GROUPS + 4,)),
            pltpu.SemaphoreType.DMA((steps, GROUPS)),
            pltpu.SemaphoreType.DMA((steps, GROUPS, 2)),
            pltpu.SemaphoreType.DMA((steps, GROUPS, 2)),
            pltpu.SemaphoreType.DMA((steps, GROUPS)),
            pltpu.SemaphoreType.DMA((3 + 2 * GROUPS, 2)),
            pltpu.SemaphoreType.DMA((3 + 2 * GROUPS, 2)),
        ],
        compiler_params=pltpu.CompilerParams(
            collective_id=0, has_side_effects=True, vmem_limit_bytes=56 * 1024 * 1024
        ),
    )(
        z_inverse[0],
        sources[:, 0],
        v_start[0],
        hist_near[:, 0],
        hist_far[:, 0],
        *small,
    )
    return result[None]


def solution(mesh):
    placed = (
        P(("zone", "sub"), "row", None),
        P(None, ("zone", "sub"), "row", None),
        P(("zone", "sub"), "row", None),
        P(None, ("zone", "sub"), "row", None),
        P(None, ("zone", "sub"), "row", None),
        P(None, ("zone", "sub"), "row"),
        P(("zone", "sub"), "row"),
        P(),
        P(),
        P(("zone", "sub"), "row", None),
        P(("zone", "sub"), "row"),
        P(("zone", "sub"), "row"),
        P(("zone", "sub"), "row"),
    )
    return jax.shard_map(
        functools.partial(local, mesh.shape["zone"], mesh.shape["sub"]),
        mesh=mesh,
        in_specs=placed,
        out_specs=P(("zone", "sub"), "row", None),
        check_vma=False,
    )
```
